256 devices in a mesh: seq: 32 (over y, z), head: 8 (over x, core).
Axes of the slice: x: 4, y: 4, z: 8, core: 2. Of those that a mesh axis runs over, the one named last changes fastest.
Arguments:
- queries: bfloat16 [32768, 2048], P('seq', 'head'), may hold values from -6 to 6
- keys: bfloat16 [32768, 2048], P('seq', 'head'), may hold values from -6 to 6
- values: bfloat16 [32768, 4096], P('seq', 'head'), may hold values from -6 to 6
- input_gate: float32 [8, 32768], P('head', 'seq'), may hold values from -6 to 86
- forget_gate: float32 [8, 32768], P('head', 'seq'), may hold values from 0 to 20
- doc_start: int32 [32768], P('seq'), may hold values from 0 to 1, as said below
- carry_memory: float32 [8, 256, 512], P('head'), may hold values from -24 to 24
- carry_norm: float32 [8, 256], P('head'), may hold values from -24 to 24
- carry_max: float32 [8], P('head'), may hold values from 2 to 86
- out_weight: bfloat16 [4096, 4096], P('seq', 'head'), may hold values from -0.09375 to 0.09375
Outputs:
- mixed: bfloat16 [32768, 4096], P('seq', 'head')
The draws below stay inside these ranges and needn't reach their ends.
Inputs may be any that keep to these rules, and one draw needn't show every extreme that they name: `doc_start`: exactly one token of the window begins a document, never the first.
All inputs are finite; a program needn't handle non-finite values.
Results may differ from the reference program's by a relative error of at most 0.019.
Values may be sent and summed in bfloat16 or wider, within the bound.
A program may use at most 128 MiB of HBM per device.

```python
import jax
import jax.numpy as jnp
from jax import lax

D = 4096
NH = 8
DK = 256
DV = 512
TOK_DEV = 1024
WINDOW_TOKENS = 32768
N_SEQ = 32


def draw_input_gate(key, part):
    key = jax.random.fold_in(key, 11)
    key_shift, key_noise = jax.random.split(key)
    shift = jax.random.uniform(key_shift, (NH, 1), jnp.float32, -2.0, 2.0)
    noise = jax.random.uniform(key_noise, (NH, WINDOW_TOKENS), jnp.float32, -4.0, 4.0)
    return shift + noise


def draw_carry_max(key, part):
    key = jax.random.fold_in(key, 12)
    lowest = 2.0
    return lowest + jax.random.uniform(key, (NH,), jnp.float32, 0.0, 4.0)


def draw_forget_gate(key, part):
    key = jax.random.fold_in(key, 13)
    every_key_row = jax.random.split(key, 7)
    share = 0.5
    quick = jax.random.uniform(every_key_row[0], (NH, 1)) < share
    slow_rate = 2.3 / WINDOW_TOKENS * jnp.exp(jax.random.uniform(every_key_row[1], (NH, 1), jnp.float32, jnp.log(0.1), jnp.log(0.6)))
    quick_rate = 1.0 / jax.random.uniform(every_key_row[2], (NH, 1), jnp.float32, 30.0, 50.0)
    rate = jnp.where(quick, quick_rate, slow_rate)
    block_factor = jnp.exp(jax.random.uniform(every_key_row[3], (NH, WINDOW_TOKENS // TOK_DEV), jnp.float32, jnp.log(0.5), jnp.log(2.0)))
    block_factor = jnp.repeat(block_factor, TOK_DEV, axis=1)
    token_factor = jnp.exp(jax.random.uniform(every_key_row[4], (NH, WINDOW_TOKENS), jnp.float32, jnp.log(0.5), jnp.log(2.0)))
    loss = rate * block_factor * token_factor
    document_runs = jax.random.randint(every_key_row[5], (3,), 0, WINDOW_TOKENS)
    boundary_hit = jnp.any(jnp.arange(WINDOW_TOKENS)[None, :] == document_runs[:, None], axis=0)
    kept = jax.random.uniform(every_key_row[6], (NH, WINDOW_TOKENS), jnp.float32, 0.5, 0.8)
    loss = jnp.where(boundary_hit[None, :], -jnp.log(kept), loss)
    return -jnp.log(jnp.expm1(loss))


def draw_doc_start(key, part):
    key = jax.random.fold_in(key, 14)
    where_start = jax.random.randint(key, (), 1, WINDOW_TOKENS)
    return (jnp.arange(WINDOW_TOKENS) == where_start).astype(jnp.int32)


def shard_levels(key, extent, cuts, low, largest):
    level = 1.0
    for axis_at, shards_of in cuts:
        draws = jax.random.uniform(jax.random.fold_in(jax.random.fold_in(key, 6), axis_at), (shards_of,), jnp.float32, low / len(cuts), largest / len(cuts))
        level = level * jnp.repeat(jnp.exp(draws), extent[axis_at] // shards_of).reshape((-1,) + (1,) * (len(extent) - 1 - axis_at))
    return level


def normal_values(stream_key, dims, width, limit, cuts=(), held_as=jnp.bfloat16):
    result = jax.random.normal(stream_key, dims, jnp.float32) * width
    if len(cuts) > 0:
        result = shard_levels(stream_key, dims, cuts, -0.22, 0.18) * result
    return jnp.clip(result, min=-limit, max=limit).astype(held_as)


def setup_inputs(seed: int = 0) -> dict:
    arg_keys = jax.random.split(jax.random.key(seed), 11)
    return {
        "queries": normal_values(arg_keys[0], (WINDOW_TOKENS, NH * DK), 1.0, 6.0, ((0, 32), (1, 8))),
        "keys": normal_values(arg_keys[1], (WINDOW_TOKENS, NH * DK), 1.0, 6.0, ((0, 32), (1, 8))),
        "values": normal_values(arg_keys[2], (WINDOW_TOKENS, NH * DV), 1.0, 6.0, ((0, 32), (1, 8))),
        "input_gate": draw_input_gate(jax.random.fold_in(arg_keys[10], 71), 0),
        "forget_gate": draw_forget_gate(jax.random.fold_in(arg_keys[10], 71), 0),
        "doc_start": draw_doc_start(jax.random.fold_in(arg_keys[10], 71), 0),
        "carry_memory": normal_values(arg_keys[6], (NH, DK, DV), 4.0, 24.0, ((0, 8),), jnp.float32),
        "carry_norm": normal_values(arg_keys[7], (NH, DK), 4.0, 24.0, ((0, 8),), jnp.float32),
        "carry_max": draw_carry_max(jax.random.fold_in(arg_keys[10], 71), 0),
        "out_weight": normal_values(arg_keys[9], (NH * DV, D), (NH * DV) ** -0.5, 0.09375, ((0, 32), (1, 8))),
    }


HIGH = lax.Precision.HIGHEST


def block_terms(queries, keys, values, input_gate, forget_gate, starts):
    steps = queries.shape[0]
    heads = queries.shape[1] // DK
    scale = DK ** -0.5
    q_three = queries.reshape(steps, heads, DK).astype(jnp.float32)
    k_three = keys.reshape(steps, heads, DK).astype(jnp.float32)
    v_three = values.reshape(steps, heads, DV).astype(jnp.float32)
    decay = jnp.cumsum(jax.nn.log_sigmoid(forget_gate), axis=1)
    segment = jnp.cumsum(starts)
    places = jnp.arange(steps)
    allowed = (places[None, :] <= places[:, None]) & (segment[None, :] == segment[:, None])
    expo = decay[:, :, None] - decay[:, None, :] + input_gate[:, None, :]
    expo = jnp.where(allowed[None], expo, -1e30)
    local_max = jnp.max(expo, axis=2)
    scores = jnp.einsum("thd,shd->hts", q_three, k_three, precision=HIGH) * scale
    weights = jnp.exp(expo - local_max[:, :, None]) * scores
    local_den = jnp.sum(weights, axis=2)
    weights_b = weights.astype(jnp.bfloat16).astype(jnp.float32)
    local_num = jnp.einsum("hts,shv->htv", weights_b, v_three, precision=HIGH)
    coeff = jnp.exp(expo[:, -1, :] - local_max[:, -1:])
    keyed = k_three * jnp.transpose(coeff)[:, :, None] * scale
    block_normalizer_sum = jnp.sum(keyed, axis=0)
    keyed_b = keyed.astype(jnp.bfloat16).astype(jnp.float32)
    block_memory = jnp.einsum("shd,shv->hdv", keyed_b, v_three, precision=HIGH)
    reset = jnp.broadcast_to((segment[-1] > 0).astype(jnp.float32), (heads,))
    summary = (block_memory, block_normalizer_sum, local_max[:, -1], decay[:, -1], reset)
    return local_num, local_den, local_max, decay, segment, summary


def combine(earlier, later):
    keep = later[4] < 0.5
    inward = earlier[2] + later[3]
    top = jnp.where(keep, jnp.maximum(inward, later[2]), later[2])
    first = jnp.where(keep, jnp.exp(jnp.minimum(inward - top, 0.0)), 0.0)
    second = jnp.exp(later[2] - top)
    memory = first[:, None, None] * earlier[0] + second[:, None, None] * later[0]
    normal = first[:, None] * earlier[1] + second[:, None] * later[1]
    return (memory, normal, top, earlier[3] + later[3], jnp.maximum(earlier[4], later[4]))


def finish(queries, local_num, local_den, local_max, decay, segment, entry):
    steps = queries.shape[0]
    heads = queries.shape[1] // DK
    q_three = queries.reshape(steps, heads, DK).astype(jnp.float32)
    fresh = (segment == 0)[None, :]
    inward = entry[2][:, None] + decay
    merged = jnp.where(fresh, jnp.maximum(inward, local_max), local_max)
    carried = jnp.where(fresh, jnp.exp(jnp.minimum(inward - merged, 0.0)), 0.0)
    own = jnp.exp(local_max - merged)
    state_numerator = jnp.einsum("thd,hdv->htv", q_three, entry[0], precision=HIGH)
    state_den = jnp.einsum("thd,hd->ht", q_three, entry[1], precision=HIGH)
    numer = own[:, :, None] * local_num + carried[:, :, None] * state_numerator
    denom = own * local_den + carried * state_den
    hidden = numer / jnp.maximum(jnp.abs(denom), 1.0)[:, :, None]
    return jnp.transpose(hidden, (1, 0, 2)).reshape(steps, heads * DV).astype(jnp.bfloat16)


def reference(queries, keys, values, input_gate, forget_gate, doc_start, carry_memory, carry_norm, carry_max, out_weight):
    q_blocks = queries.reshape(N_SEQ, TOK_DEV, NH * DK)
    k_blocks = keys.reshape(N_SEQ, TOK_DEV, NH * DK)
    v_blocks = values.reshape(N_SEQ, TOK_DEV, NH * DV)
    i_blocks = jnp.transpose(input_gate.reshape(NH, N_SEQ, TOK_DEV), (1, 0, 2))
    f_blocks = jnp.transpose(forget_gate.reshape(NH, N_SEQ, TOK_DEV), (1, 0, 2))
    s_blocks = doc_start.reshape(N_SEQ, TOK_DEV)
    start_state = (carry_memory, carry_norm, carry_max, jnp.zeros((NH,), jnp.float32), jnp.ones((NH,), jnp.float32))

    def advance(state, block):
        q_block, k_block, value_block, i_block, forget_block, s_block = block
        local_num, local_den, local_max, decay, segment, summary = block_terms(q_block, k_block, value_block, i_block, forget_block, s_block)
        hidden = finish(q_block, local_num, local_den, local_max, decay, segment, state)
        return combine(state, summary), hidden

    unused, hiddens = lax.scan(advance, start_state, (q_blocks, k_blocks, v_blocks, i_blocks, f_blocks, s_blocks))
    hidden = hiddens.reshape(WINDOW_TOKENS, NH * DV)
    return jnp.dot(hidden, out_weight, preferred_element_type=jnp.float32).astype(jnp.bfloat16)
```

```python
import jax
import jax.numpy as jnp
from jax import lax
from jax.experimental import pallas as pl
from jax.experimental.pallas import tpu as pltpu
from jax.sharding import PartitionSpec as P

DK = 256
DV = 512
TOK = 1024
NY, NZ = 4, 8
NS = NY * NZ
LOW = -1e30
MESH = pl.DeviceIdType.MESH
F32, BF16 = jnp.float32, jnp.bfloat16
QT = 256
XT = 128
NXT = TOK // XT


def lane_scan(a, op, fill, seg=None):
    lane = lax.broadcasted_iota(jnp.int32, a.shape, 1)
    for sh in (1, 2, 4, 8, 16, 32, 64):
        ok = lane >= sh
        if seg is not None:
            ok = ok & (pltpu.roll(seg, sh, 1) == seg)
        a = op(a, jnp.where(ok, pltpu.roll(a, sh, 1), fill))
    return a


def row_scan(a, op, fill, seg=None):
    row = lax.broadcasted_iota(jnp.int32, a.shape, 0)
    for sh in (1, 2, 4):
        ok = row >= sh
        if seg is not None:
            ok = ok & (pltpu.roll(seg, sh, 0) == seg)
        a = op(a, jnp.where(ok, pltpu.roll(a, sh, 0), fill))
    return a


def last_lane(a):
    return jnp.broadcast_to(a[:, 127:128], a.shape)


def before(a, fill):
    row = lax.broadcasted_iota(jnp.int32, a.shape, 0)
    return jnp.where(row >= 1, pltpu.roll(a, 1, 0), fill)


def running_sum(a):
    inside = lane_scan(a, jnp.add, 0.0)
    return inside + before(row_scan(last_lane(inside), jnp.add, 0.0), 0.0)


def running_max(a, seg):
    inside = lane_scan(a, jnp.maximum, LOW, seg)
    seg_end = last_lane(seg)
    ends = row_scan(last_lane(inside), jnp.maximum, LOW, seg_end)
    carried = jnp.where(before(seg_end, -1.0) == seg, before(ends, LOW), LOW)
    return jnp.maximum(inside, carried)


def column(cols, tile, size):
    per = size // 128
    return jnp.concatenate([cols[:, tile * per + i : tile * per + i + 1] for i in range(per)], 0)


def as_row(a, rows):
    return jnp.concatenate([a[i : i + 1, :] for i in range(rows)], 1)


def kernel(
    q_ref, k_ref, v_ref, ig_ref, fg_ref, ds_ref, cmem_ref, cnorm_ref, cmax_ref, w_ref,
    out_ref,
    wbuf, stats, cpack, crecv, epack, erecv, num, den, hid, part_out, part_in, acc, gates,
    wsend, wrecv, swap_send, ssend, srecv, csend, crecv_sem, esend, erecv_sem,
    hsend, hrecv, psend, precv,
):
    me = lax.axis_index("seq")
    head = lax.axis_index("head")
    y, z = me // NZ, me % NZ
    x, core = head // 2, head % 2
    mate = 1 - core
    near = (x // 2) * 2 + (1 - x % 2)
    far = 3 - x
    home = (y // 2) == (x // 2)
    swap_seq = ((y + 2) % NY) * NZ + z

    def at(yy, zz):
        return ((yy + NY) % NY) * NZ + (zz + NZ) % NZ

    barrier = pltpu.get_barrier_semaphore()

    def greet(seq, hd):
        pl.semaphore_signal(
            barrier, inc=1, device_id={"seq": seq, "head": hd}, device_id_type=MESH
        )

    def greet_seq(d, c):
        greet((me + d) % NS, head)
        return c

    lax.fori_loop(1, NS, greet_seq, 0)
    greet(me, x * 2 + mate)
    greet(me, near * 2 + core)
    greet(me, far * 2 + core)

    @pl.when(jnp.logical_not(home))
    def _():
        greet(swap_seq, far * 2 + core)

    def w_copy(slot, dev):
        return pltpu.make_async_remote_copy(
            src_ref=wbuf.at[slot], dst_ref=wbuf.at[slot], send_sem=wsend,
            recv_sem=wrecv.at[slot], device_id={"seq": dev, "head": head},
            device_id_type=MESH,
        )

    def swap_copy():
        return pltpu.make_async_remote_copy(
            src_ref=w_ref, dst_ref=wbuf.at[swap_seq], send_sem=swap_send,
            recv_sem=wrecv.at[swap_seq], device_id={"seq": swap_seq, "head": far * 2 + core},
            device_id_type=MESH,
        )

    def w_sends(slot, zs, ys):
        for dz in zs:
            w_copy(slot, at(y, z + dz)).start()
        for dy in ys:
            w_copy(slot, at(y + dy, z)).start()

    def w_wait(slot):
        w_copy(slot, me).wait_recv()

    lf = fg_ref[...]
    lf = jnp.minimum(lf, 0.0) - jnp.log1p(jnp.exp(-jnp.abs(lf)))
    decay = running_sum(lf)
    seg = running_sum(ds_ref[...].astype(F32))
    u = ig_ref[...] - decay
    top = running_max(u, seg)
    local_max = decay + top
    end = lambda a: jnp.broadcast_to(a[7:8, 127:128], (1, 128))
    seg_end = end(seg)
    coeff = jnp.where(seg == seg_end, jnp.exp(jnp.minimum(u - end(top), 0.0)), 0.0) * (DK**-0.5)
    coeff_cols = jnp.transpose(coeff)
    top_cols = jnp.transpose(top)
    seg_cols = jnp.transpose(seg)
    keyed = [
        k_ref[i * 128 : (i + 1) * 128, :].astype(F32) * coeff_cols[:, i : i + 1] for i in range(8)
    ]
    normal = sum(jnp.sum(t, axis=0, keepdims=True) for t in keyed)
    stats[me, 0:1, :] = normal[:, :128]
    stats[me, 1:2, :] = normal[:, 128:]
    stats[me, 2:3, :] = end(local_max)
    stats[me, 3:4, :] = end(decay)
    stats[me, 4:5, :] = jnp.where(seg_end > 0.5, 1.0, 0.0)

    waits = jnp.where(home, 34, 35)
    pl.semaphore_wait(barrier, waits)

    @pl.when(home)
    def _():
        wbuf[me] = w_ref[...]
        w_sends(me, (1, -1), (1, -1))

    @pl.when(jnp.logical_not(home))
    def _():
        swap_copy().start()

    def stats_copy(dev):
        return pltpu.make_async_remote_copy(
            src_ref=stats.at[me], dst_ref=stats.at[me], send_sem=ssend, recv_sem=srecv,
            device_id={"seq": dev, "head": head}, device_id_type=MESH,
        )

    def send_stats(d, c):
        stats_copy((me + d) % NS).start()
        return c

    lax.fori_loop(1, NS, send_stats, 0)

    memory = lax.dot_general(
        jnp.concatenate([t.astype(BF16) for t in keyed], 0), v_ref[...],
        (((0,), (0,)), ((), ())), preferred_element_type=F32,
    ).astype(BF16)
    cpack[0:16] = memory[:, :256].reshape(16, 16, 256)
    cpack[16:32] = memory[:, 256:].reshape(16, 16, 256)
    crecv[me] = cpack[me]

    def c_copy(dev):
        return pltpu.make_async_remote_copy(
            src_ref=cpack.at[dev], dst_ref=crecv.at[me], send_sem=csend, recv_sem=crecv_sem,
            device_id={"seq": dev, "head": head}, device_id_type=MESH,
        )

    def send_c(d, c):
        c_copy((me + d) % NS).start()
        return c

    lax.fori_loop(1, NS, send_c, 0)

    @pl.when(jnp.logical_not(home))
    def _():
        swap_copy().wait_send()
        w_wait(me)
        w_sends(me, (1, -1), (1, -1))

    def attend(tile):
        n = (tile + 1) * QT
        qt = q_ref[tile * QT : (tile + 1) * QT, :]
        scores = lax.dot_general(
            qt, k_ref[:n, :], (((1,), (1,)), ((), ())), preferred_element_type=F32
        )
        blocks = n // 128
        u_row, seg_row = as_row(u, blocks), as_row(seg, blocks)
        place = lax.broadcasted_iota(jnp.int32, (QT, n), 0) + tile * QT
        allowed = (lax.broadcasted_iota(jnp.int32, (QT, n), 1) <= place) & (
            seg_row == column(seg_cols, tile, QT)
        )
        gain = jnp.exp(u_row - column(top_cols, tile, QT))
        weights = jnp.where(allowed, gain * (DK**-0.5), 0.0) * scores
        den[tile * QT : (tile + 1) * QT, :] = jnp.sum(weights, axis=1, keepdims=True)
        num[tile * QT : (tile + 1) * QT, :] = jnp.dot(
            weights.astype(BF16), v_ref[:n, :], preferred_element_type=F32
        )

    def z_step(k):
        w_wait(at(y, z - k))
        w_sends(at(y, z - k), (1,) if k <= 3 else (), (1, -1))
        if k <= 3:
            w_wait(at(y, z + k))
            w_sends(at(y, z + k), (-1,) if k <= 2 else (), (1, -1))

    def y_step(o, up):
        w_wait(at(y - 1, z + o))
        w_wait(at(y + 1, z + o))
        if up:
            w_sends(at(y - 1, z + o), (), (1,))
        else:
            w_sends(at(y + 1, z + o), (), (-1,))

    attend(0)
    z_step(1)
    attend(1)
    attend(2)
    z_step(2)
    attend(3)

    def all_pieces(ref, sem):
        part = ref.at[pl.ds(0, NS - 1)]
        return pltpu.make_async_copy(part, part, sem)

    all_pieces(stats, srecv).wait()
    m = jnp.broadcast_to(cmax_ref[...], (1, 128))
    n0, n1 = cnorm_ref[0:1, :], cnorm_ref[1:2, :]
    em, e0, e1 = m, n0, n1
    firsts, seconds = [], []
    for j in range(NS - 1):
        keep = stats[j, 4:5, :] < 0.5
        inward = m + stats[j, 3:4, :]
        later = stats[j, 2:3, :]
        m = jnp.where(keep, jnp.maximum(inward, later), later)
        first = jnp.where(keep, jnp.exp(jnp.minimum(inward - m, 0.0)), 0.0)
        second = jnp.exp(later - m)
        n0 = first * n0 + second * stats[j, 0:1, :]
        n1 = first * n1 + second * stats[j, 1:2, :]
        here = me == j + 1
        em, e0, e1 = (jnp.where(here, b, a) for a, b in ((em, m), (e0, n0), (e1, n1)))
        gates[j, 0:1, :] = first
        gates[j, 1:2, :] = second

    group, half = me % 16, me // 16
    carry_rows = cmem_ref[pl.ds(pl.multiple_of(group * 16, 16), 16), :]
    state = jnp.where(half == 0, carry_rows[:, :256], carry_rows[:, 256:])
    all_pieces(crecv, crecv_sem).wait()
    epack[0] = state.astype(BF16)
    for j in range(NS - 1):
        first = jnp.concatenate([gates[j, 0:1, :]] * 2, 1)
        second = jnp.concatenate([gates[j, 1:2, :]] * 2, 1)
        state = first * state + second * crecv[j].astype(F32)
        epack[j + 1] = state.astype(BF16)
    erecv[me] = epack[me]

    def e_copy(dev):
        return pltpu.make_async_remote_copy(
            src_ref=epack.at[dev], dst_ref=erecv.at[me], send_sem=esend, recv_sem=erecv_sem,
            device_id={"seq": dev, "head": head}, device_id_type=MESH,
        )

    def send_e(d, c):
        e_copy((me + d) % NS).start()
        return c

    lax.fori_loop(1, NS, send_e, 0)
    z_step(3)

    inward = jnp.broadcast_to(em, (8, 128)) + decay
    fresh = seg < 0.5
    merged = jnp.where(fresh, jnp.maximum(inward, local_max), local_max)
    carried = jnp.where(fresh, jnp.exp(jnp.minimum(inward - merged, 0.0)), 0.0)
    own = jnp.exp(local_max - merged)
    carried_cols, own_cols = jnp.transpose(carried), jnp.transpose(own)
    en = jnp.concatenate([e0, e1], 1)
    high = en.astype(BF16)
    rest = en - high.astype(F32)
    mid = rest.astype(BF16)
    low = (rest - mid.astype(F32)).astype(BF16)
    norms = jnp.concatenate(
        [high.astype(F32), mid.astype(F32), low.astype(F32), jnp.zeros((5, DK), F32)], 0
    ).astype(BF16)
    sden = lax.dot_general(
        q_ref[...], norms, (((1,), (1,)), ((), ())), preferred_element_type=F32
    )
    sden = jnp.sum(sden, axis=1, keepdims=True)
    for i in range(8):
        rows = slice(i * 128, (i + 1) * 128)
        o, c = own_cols[:, i : i + 1], carried_cols[:, i : i + 1]
        whole = o * den[rows, :] + c * sden[rows, :]
        inverse = 1.0 / jnp.maximum(jnp.abs(whole), 1.0)
        den[rows, :] = c * inverse
        num[rows, :] = num[rows, :] * (o * inverse)

    z_step(4)
    all_pieces(erecv, erecv_sem).wait()
    entry_a = erecv[0:16].reshape(256, 256)
    entry_b = erecv[16:32].reshape(256, 256)
    mine, theirs = (x % 2) * 2 + core, (x % 2) * 2 + mate
    other, other_mate = (1 - x % 2) * 2 + core, (1 - x % 2) * 2 + mate

    def rows_of(t):
        return pl.ds(pl.multiple_of(t * XT, XT), XT)

    def h_copy(slot, t, hd):
        return pltpu.make_async_remote_copy(
            src_ref=hid.at[slot, rows_of(t)], dst_ref=hid.at[slot, rows_of(t)], send_sem=hsend,
            recv_sem=hrecv.at[slot, t], device_id={"seq": me, "head": hd}, device_id_type=MESH,
        )

    def make_hidden(t, c):
        rows = rows_of(t)
        qt = q_ref[rows, :]
        scale = den[rows, :]
        for part, e in ((slice(0, 256), entry_a), (slice(256, 512), entry_b)):
            got = jnp.dot(qt, e, preferred_element_type=F32)
            hid[mine, rows, part] = (num[rows, part] + scale * got).astype(BF16)
        h_copy(mine, t, near * 2 + core).start()
        h_copy(mine, t, x * 2 + mate).start()
        return c

    lax.fori_loop(0, NXT, make_hidden, 0)

    order = ((0, True), (-1, True), (1, False), (-2, False), (2, True), (-3, True), (3, False), (-4, False))
    for o, up in order:
        y_step(o, up)
    for o, _ in order:
        w_wait(at(y + 2, z + o))

    def p_copy(t):
        return pltpu.make_async_remote_copy(
            src_ref=part_out.at[rows_of(t)], dst_ref=part_in.at[rows_of(t)], send_sem=psend,
            recv_sem=precv.at[t], device_id={"seq": me, "head": far * 2 + core},
            device_id_type=MESH,
        )

    own_base, far_base = 16 * (x // 2), 16 * (1 - x // 2)

    def project(t, base):
        total = None
        for j in range(4):
            w = wbuf[pl.ds(base + 4 * j, 4)].reshape(DV, DV)
            term = jnp.dot(hid[j, rows_of(t), :], w, preferred_element_type=F32)
            total = term if total is None else total + term
        return total

    def cross(t, c):
        h_copy(other, t, head).wait_recv()
        h_copy(other, t, x * 2 + mate).start()
        h_copy(theirs, t, head).wait_recv()
        h_copy(other_mate, t, head).wait_recv()
        part_out[rows_of(t), :] = project(t, far_base).astype(BF16)
        p_copy(t).start()
        acc[rows_of(t), :] = project(t, own_base)
        return c

    lax.fori_loop(0, NXT, cross, 0)

    def finish(t, c):
        p_copy(t).wait_recv()
        rows = rows_of(t)
        out_ref[rows, :] = (acc[rows, :] + part_in[rows, :].astype(F32)).astype(BF16)
        return c

    lax.fori_loop(0, NXT, finish, 0)

    all_pieces(wbuf, wsend).wait()
    all_pieces(stats, ssend).wait()
    all_pieces(cpack, csend).wait()
    all_pieces(epack, esend).wait()
    whole = hid.at[pl.ds(0, 3)]
    pltpu.make_async_copy(whole, whole, hsend).wait()
    pltpu.make_async_copy(part_out, part_out, psend).wait()


def shards(q, k, v, ig, fg, ds, cmem, cnorm, cmax, w):
    dma = pltpu.SemaphoreType.DMA
    vmem = pl.BlockSpec(memory_space=pltpu.VMEM)
    return pl.pallas_call(
        kernel,
        out_shape=jax.ShapeDtypeStruct((TOK, DV), BF16),
        in_specs=[vmem] * 10,
        out_specs=vmem,
        scratch_shapes=[
            pltpu.VMEM((NS, 128, DV), BF16),
            pltpu.VMEM((NS, 8, 128), F32),
            pltpu.VMEM((NS, 16, 256), BF16),
            pltpu.VMEM((NS, 16, 256), BF16),
            pltpu.VMEM((NS, 16, 256), BF16),
            pltpu.VMEM((NS, 16, 256), BF16),
            pltpu.VMEM((TOK, DV), F32),
            pltpu.VMEM((TOK, 1), F32),
            pltpu.VMEM((4, TOK, DV), BF16),
            pltpu.VMEM((TOK, DV), BF16),
            pltpu.VMEM((TOK, DV), BF16),
            pltpu.VMEM((TOK, DV), F32),
            pltpu.VMEM((NS, 8, 128), F32),
            dma, dma((NS,)), dma, dma, dma, dma, dma, dma, dma,
            dma, dma((4, NXT)), dma, dma((NXT,)),
        ],
        compiler_params=pltpu.CompilerParams(
            collective_id=0, has_side_effects=True, vmem_limit_bytes=56 * 2**20
        ),
    )(
        q, k, v, ig.reshape(8, 128), fg.reshape(8, 128), ds.reshape(8, 128),
        cmem.reshape(DK, DV), cnorm.reshape(2, 128), cmax.reshape(1, 1), w,
    )


def solution(mesh):
    placed = (
        P("seq", "head"),
        P("seq", "head"),
        P("seq", "head"),
        P("head", "seq"),
        P("head", "seq"),
        P("seq"),
        P("head", None, None),
        P("head", None),
        P("head"),
        P("seq", "head"),
    )
    return jax.shard_map(
        shards, mesh=mesh, in_specs=placed, out_specs=P("seq", "head"), check_vma=False
    )
```

```python
import jax
import jax.numpy as jnp
from jax import lax
from jax.experimental import pallas as pl
from jax.experimental.pallas import tpu as pltpu
from jax.sharding import PartitionSpec as P

DK = 256
DV = 512
TOK = 1024
NY, NZ = 4, 8
NS = NY * NZ
LOW = -1e30
MESH = pl.DeviceIdType.MESH
F32, BF16 = jnp.float32, jnp.bfloat16
QT = 256
XT = 128
NXT = TOK // XT


def lane_scan(a, op, fill, seg=None):
    lane = lax.broadcasted_iota(jnp.int32, a.shape, 1)
    for sh in (1, 2, 4, 8, 16, 32, 64):
        ok = lane >= sh
        if seg is not None:
            ok = ok & (pltpu.roll(seg, sh, 1) == seg)
        a = op(a, jnp.where(ok, pltpu.roll(a, sh, 1), fill))
    return a


def row_scan(a, op, fill, seg=None):
    row = lax.broadcasted_iota(jnp.int32, a.shape, 0)
    for sh in (1, 2, 4):
        ok = row >= sh
        if seg is not None:
            ok = ok & (pltpu.roll(seg, sh, 0) == seg)
        a = op(a, jnp.where(ok, pltpu.roll(a, sh, 0), fill))
    return a


def last_lane(a):
    return jnp.broadcast_to(a[:, 127:128], a.shape)


def before(a, fill):
    row = lax.broadcasted_iota(jnp.int32, a.shape, 0)
    return jnp.where(row >= 1, pltpu.roll(a, 1, 0), fill)


def running_sum(a):
    inside = lane_scan(a, jnp.add, 0.0)
    return inside + before(row_scan(last_lane(inside), jnp.add, 0.0), 0.0)


def running_max(a, seg):
    inside = lane_scan(a, jnp.maximum, LOW, seg)
    seg_end = last_lane(seg)
    ends = row_scan(last_lane(inside), jnp.maximum, LOW, seg_end)
    carried = jnp.where(before(seg_end, -1.0) == seg, before(ends, LOW), LOW)
    return jnp.maximum(inside, carried)


def column(cols, tile, size):
    per = size // 128
    return jnp.concatenate([cols[:, tile * per + i : tile * per + i + 1] for i in range(per)], 0)


def as_row(a, rows):
    return jnp.concatenate([a[i : i + 1, :] for i in range(rows)], 1)


def kernel(
    q_hbm, k_hbm, v_hbm, ig_ref, fg_ref, ds_ref, cmem_hbm, cnorm_ref, cmax_ref, w_hbm,
    out_ref,
    q_ref, k_ref, v_ref, cmem_ref,
    wfar, wown, stats, cpack, crecv, epack, erecv, num, den, hid, part_out, part_in, gates,
    in_sem, fsend, frecv, osend, orecv, oring, swap_send, ssend, srecv, srecv_rows,
    csend, crecv_sem, esend, erecv_sem, hsend, hrecv, psend, precv,
):
    me = lax.axis_index("seq")
    head = lax.axis_index("head")
    y, z = me // NZ, me % NZ
    x, core = head // 2, head % 2
    mate = 1 - core
    near = (x // 2) * 2 + (1 - x % 2)
    far = 3 - x
    home = (y // 2) == (x // 2)
    away = jnp.logical_not(home)
    opposite = ((y + 2) % NY) * NZ + z
    far_head = far * 2 + core

    def at(yy, zz):
        return ((yy + NY) % NY) * NZ + (zz + NZ) % NZ

    barrier = pltpu.get_barrier_semaphore()

    def greet(seq, hd):
        pl.semaphore_signal(
            barrier, inc=1, device_id={"seq": seq, "head": hd}, device_id_type=MESH
        )

    for d in range(1, NS):
        greet((me + d) % NS, head)
    greet(me, x * 2 + mate)
    greet(me, near * 2 + core)
    greet(me, far_head)

    @pl.when(away)
    def _():
        greet(opposite, far_head)

    loads = [
        pltpu.make_async_copy(a, b, in_sem.at[i])
        for i, (a, b) in enumerate(
            ((k_hbm, k_ref), (v_hbm, v_ref), (q_hbm, q_ref), (cmem_hbm, cmem_ref))
        )
    ]
    for load in loads:
        load.start()

    def remote(src, dst, send, recv, seq, hd):
        return pltpu.make_async_remote_copy(
            src_ref=src, dst_ref=dst, send_sem=send, recv_sem=recv,
            device_id={"seq": seq, "head": hd}, device_id_type=MESH,
        )

    def total(ref, count, sem):
        part = ref.at[pl.ds(0, count)]
        return pltpu.make_async_copy(part, part, sem)

    lf = fg_ref[...]
    lf = jnp.minimum(lf, 0.0) - jnp.log1p(jnp.exp(-jnp.abs(lf)))
    decay = running_sum(lf)
    seg = running_sum(ds_ref[...].astype(F32))
    u = ig_ref[...] - decay
    top = running_max(u, seg)
    local_max = decay + top
    end = lambda a: jnp.broadcast_to(a[7:8, 127:128], (1, 128))
    seg_end = end(seg)
    coeff = jnp.where(seg == seg_end, jnp.exp(jnp.minimum(u - end(top), 0.0)), 0.0) * (DK**-0.5)
    coeff_cols = jnp.transpose(coeff)
    top_cols = jnp.transpose(top)
    seg_cols = jnp.transpose(seg)

    loads[0].wait()
    keyed = [
        k_ref[i * 128 : (i + 1) * 128, :].astype(F32) * coeff_cols[:, i : i + 1] for i in range(8)
    ]
    normal = sum(jnp.sum(t, axis=0, keepdims=True) for t in keyed)
    stats[me, 0:1, :] = normal[:, :128]
    stats[me, 1:2, :] = normal[:, 128:]
    stats[me, 2:3, :] = end(local_max)
    stats[me, 3:4, :] = end(decay)
    stats[me, 4:5, :] = jnp.where(seg_end > 0.5, 1.0, 0.0)
    loads[1].wait()
    memory = lax.dot_general(
        jnp.concatenate([t.astype(BF16) for t in keyed], 0), v_ref[...],
        (((0,), (0,)), ((), ())), preferred_element_type=F32,
    ).astype(BF16)
    cpack[0:16] = memory[:, :256].reshape(16, 16, 256)
    cpack[16:32] = memory[:, 256:].reshape(16, 16, 256)
    crecv[me] = cpack[me]

    pl.semaphore_wait(barrier, jnp.where(home, 34, 35))

    mine_row = (y % 2) * NZ + z
    upper, lower = w_hbm.at[pl.ds(0, 64)], w_hbm.at[pl.ds(64, 64)]
    first, second = 2 * mine_row, 2 * mine_row + 1
    stay = pltpu.make_async_copy(upper, wown.at[first], in_sem.at[4])

    @pl.when(home)
    def _():
        stay.start()
        remote(lower, wown.at[second], swap_send, orecv.at[opposite], opposite, head).start()

    @pl.when(away)
    def _():
        remote(upper, wfar.at[first], swap_send, frecv.at[me], me, far_head).start()
        remote(lower, wfar.at[second], swap_send, frecv.at[opposite], opposite, far_head).start()

    for d in range(1, NS):
        dev = (me + d) % NS
        remote(cpack.at[dev], crecv.at[me], csend, crecv_sem, dev, head).start()
    for d in range(1, NZ):
        remote(stats.at[me], stats.at[me], ssend, srecv, at(y, z + d), head).start()

    def place(yy, zz):
        yy = (yy + NY) % NY
        half = jnp.where((yy // 2) == (x // 2), 0, 1)
        return ((yy % 2) * NZ + (zz + NZ) % NZ) * 2 + half

    def f_copy(yy, zz, dev):
        piece = wfar.at[place(yy, zz)]
        return remote(piece, piece, fsend, frecv.at[at(yy, zz)], dev, head)

    def o_copy(yy, dev):
        piece = wown.at[place(yy, z)]
        return remote(piece, piece, osend, orecv.at[at(yy, z)], dev, head)

    def r_copy(a, zz, dev):
        row = a * NZ + (zz + NZ) % NZ
        piece = wown.at[pl.ds(row * 2, 2)]
        return remote(piece, piece, osend, oring.at[row], dev, head)

    def f_sends(yy, zz, zs, ys):
        for dz in zs:
            f_copy(yy, zz, at(y, z + dz)).start()
        for dy in ys:
            f_copy(yy, zz, at(y + dy, z)).start()

    def z_step(k):
        f_copy(y, z - k, me).wait_recv()
        f_sends(y, z - k, (1,) if k <= 3 else (), (1, -1))
        if k <= 3:
            f_copy(y, z + k, me).wait_recv()
            f_sends(y, z + k, (-1,) if k <= 2 else (), (1, -1))

    def y_step(o, up):
        f_copy(y - 1, z + o, me).wait_recv()
        f_copy(y + 1, z + o, me).wait_recv()
        if up:
            f_sends(y - 1, z + o, (), (1,))
        else:
            f_sends(y + 1, z + o, (), (-1,))

    def attend(tile):
        n = (tile + 1) * QT
        qt = q_ref[tile * QT : (tile + 1) * QT, :]
        scores = lax.dot_general(
            qt, k_ref[:n, :], (((1,), (1,)), ((), ())), preferred_element_type=F32
        )
        blocks = n // 128
        u_row, seg_row = as_row(u, blocks), as_row(seg, blocks)
        spot = lax.broadcasted_iota(jnp.int32, (QT, n), 0) + tile * QT
        allowed = (lax.broadcasted_iota(jnp.int32, (QT, n), 1) <= spot) & (
            seg_row == column(seg_cols, tile, QT)
        )
        gain = jnp.exp(u_row - column(top_cols, tile, QT))
        weights = jnp.where(allowed, gain * (DK**-0.5), 0.0) * scores
        den[tile * QT : (tile + 1) * QT, :] = jnp.sum(weights, axis=1, keepdims=True)
        num[tile * QT : (tile + 1) * QT, :] = jnp.dot(
            weights.astype(BF16), v_ref[:n, :], preferred_element_type=F32
        )

    loads[2].wait()
    attend(0)
    f_copy(y, z, me).wait_recv()
    f_sends(y, z, (1, -1), (1, -1))
    attend(1)
    total(stats, NZ - 1, srecv).wait()
    row = stats.at[pl.ds(pl.multiple_of(y * NZ, NZ), NZ)]
    for dy in (1, 2, 3):
        remote(row, row, ssend, srecv_rows, at(y + dy, z), head).start()

    @pl.when(home)
    def _():
        stay.wait()
        remote(lower, wown.at[second], swap_send, orecv.at[opposite], opposite, head).wait_send()

    @pl.when(away)
    def _():
        pltpu.make_async_copy(w_hbm, w_hbm, swap_send).wait()
        o_copy(y, me).wait_recv()

    for dy in (1, -1):
        o_copy(y, at(y + dy, z)).start()
    attend(2)
    z_step(1)
    attend(3)

    loads[3].wait()
    total(stats, NS - NZ, srecv_rows).wait()
    m = jnp.broadcast_to(cmax_ref[...], (1, 128))
    n0, n1 = cnorm_ref[0:1, :], cnorm_ref[1:2, :]
    em, e0, e1 = m, n0, n1
    for j in range(NS - 1):
        keep = stats[j, 4:5, :] < 0.5
        inward = m + stats[j, 3:4, :]
        later = stats[j, 2:3, :]
        m = jnp.where(keep, jnp.maximum(inward, later), later)
        old = jnp.where(keep, jnp.exp(jnp.minimum(inward - m, 0.0)), 0.0)
        new = jnp.exp(later - m)
        n0 = old * n0 + new * stats[j, 0:1, :]
        n1 = old * n1 + new * stats[j, 1:2, :]
        here = me == j + 1
        em, e0, e1 = (jnp.where(here, b, a) for a, b in ((em, m), (e0, n0), (e1, n1)))
        gates[j, 0:1, :] = old
        gates[j, 1:2, :] = new

    inward = jnp.broadcast_to(em, (8, 128)) + decay
    fresh = seg < 0.5
    merged = jnp.where(fresh, jnp.maximum(inward, local_max), local_max)
    carried = jnp.where(fresh, jnp.exp(jnp.minimum(inward - merged, 0.0)), 0.0)
    own = jnp.exp(local_max - merged)
    carried_cols, own_cols = jnp.transpose(carried), jnp.transpose(own)
    en = jnp.concatenate([e0, e1], 1)
    high = en.astype(BF16)
    rest = en - high.astype(F32)
    mid = rest.astype(BF16)
    low = (rest - mid.astype(F32)).astype(BF16)
    norms = jnp.concatenate(
        [high.astype(F32), mid.astype(F32), low.astype(F32), jnp.zeros((5, DK), F32)], 0
    ).astype(BF16)
    sden = lax.dot_general(
        q_ref[...], norms, (((1,), (1,)), ((), ())), preferred_element_type=F32
    )
    sden = jnp.sum(sden, axis=1, keepdims=True)
    for i in range(8):
        rows = slice(i * 128, (i + 1) * 128)
        o, c = own_cols[:, i : i + 1], carried_cols[:, i : i + 1]
        whole = o * den[rows, :] + c * sden[rows, :]
        inverse = 1.0 / jnp.maximum(jnp.abs(whole), 1.0)
        den[rows, :] = c * inverse
        num[rows, :] = num[rows, :] * (o * inverse)
    z_step(2)

    group, half = me % 16, me // 16
    carry_rows = cmem_ref[pl.ds(pl.multiple_of(group * 16, 16), 16), :]
    state = jnp.where(half == 0, carry_rows[:, :256], carry_rows[:, 256:])
    total(crecv, NS - 1, crecv_sem).wait()
    epack[0] = state.astype(BF16)
    for j in range(NS - 1):
        old = jnp.concatenate([gates[j, 0:1, :]] * 2, 1)
        new = jnp.concatenate([gates[j, 1:2, :]] * 2, 1)
        state = old * state + new * crecv[j].astype(F32)
        epack[j + 1] = state.astype(BF16)
    erecv[me] = epack[me]
    for d in range(1, NS):
        dev = (me + d) % NS
        remote(epack.at[dev], erecv.at[me], esend, erecv_sem, dev, head).start()

    z_step(3)
    z_step(4)
    o_copy(y - 1, me).wait_recv()
    o_copy(y + 1, me).wait_recv()
    lift = z % 2 == 0
    o_copy(jnp.where(lift, y + 3, y + 1), at(jnp.where(lift, y + 1, y + 3), z)).start()
    order = (
        (0, True), (-1, True), (1, False), (-2, False),
        (2, True), (-3, True), (3, False), (-4, False),
    )
    for o, up in order:
        y_step(o, up)

    total(erecv, NS - 1, erecv_sem).wait()
    entry_a = erecv[0:16].reshape(256, 256)
    entry_b = erecv[16:32].reshape(256, 256)
    mine, theirs = (x % 2) * 2 + core, (x % 2) * 2 + mate
    other, other_mate = (1 - x % 2) * 2 + core, (1 - x % 2) * 2 + mate

    def rows_of(t):
        return pl.ds(pl.multiple_of(t * XT, XT), XT)

    def h_copy(slot, t, hd):
        tile = hid.at[slot, rows_of(t)]
        return remote(tile, tile, hsend, hrecv.at[slot, t], me, hd)

    def make_hidden(t, c):
        rows = rows_of(t)
        qt = q_ref[rows, :]
        scale = den[rows, :]
        for part, e in ((slice(0, 256), entry_a), (slice(256, 512), entry_b)):
            got = jnp.dot(qt, e, preferred_element_type=F32)
            hid[mine, rows, part] = (num[rows, part] + scale * got).astype(BF16)
        h_copy(mine, t, near * 2 + core).start()
        h_copy(mine, t, x * 2 + mate).start()
        return c

    lax.fori_loop(0, NXT, make_hidden, 0)

    o_copy(y + 2, me).wait_recv()
    for a in (0, 1):
        for dz in (1, -1):
            r_copy(a, z, at(y, z + dz)).start()
    for o, _ in order:
        f_copy(y + 2, z + o, me).wait_recv()

    def p_copy(t):
        return remote(
            part_out.at[rows_of(t)], part_in.at[rows_of(t)], psend, precv.at[t], me, far_head
        )

    def project(t, w_ref):
        whole = None
        for j in range(4):
            w = w_ref[8 * j : 8 * j + 8].reshape(DV, DV)
            term = jnp.dot(hid[j, rows_of(t), :], w, preferred_element_type=F32)
            whole = term if whole is None else whole + term
        return whole

    def ring_step(t):
        k, a = t // 2 + 1, t % 2

        @pl.when(k <= 4 - a)
        def _():
            r_copy(a, z - k, me).wait_recv()

        @pl.when(k <= 3 - a)
        def _():
            r_copy(a, z - k, at(y, z + 1)).start()

        @pl.when(k <= 3 + a)
        def _():
            r_copy(a, z + k, me).wait_recv()

        @pl.when(k <= 2 + a)
        def _():
            r_copy(a, z + k, at(y, z - 1)).start()

    def cross(t, c):
        h_copy(other, t, head).wait_recv()
        h_copy(other, t, x * 2 + mate).start()
        h_copy(theirs, t, head).wait_recv()
        h_copy(other_mate, t, head).wait_recv()
        part_out[rows_of(t), :] = project(t, wfar).astype(BF16)
        p_copy(t).start()
        ring_step(t)
        return c

    lax.fori_loop(0, NXT, cross, 0)

    def finish(t, c):
        kept = project(t, wown)
        p_copy(t).wait_recv()
        rows = rows_of(t)
        out_ref[rows, :] = (kept + part_in[rows, :].astype(F32)).astype(BF16)
        return c

    lax.fori_loop(0, NXT, finish, 0)

    total(wfar, 31, fsend).wait()
    total(wown, 31, osend).wait()
    total(stats, 31, ssend).wait()
    total(cpack, 31, csend).wait()
    total(epack, 31, esend).wait()
    total(hid, 3, hsend).wait()
    pltpu.make_async_copy(part_out, part_out, psend).wait()


def shards(q, k, v, ig, fg, ds, cmem, cnorm, cmax, w):
    dma = pltpu.SemaphoreType.DMA
    vmem = pl.BlockSpec(memory_space=pltpu.VMEM)
    hbm = pl.BlockSpec(memory_space=pl.ANY)
    return pl.pallas_call(
        kernel,
        out_shape=jax.ShapeDtypeStruct((TOK, DV), BF16),
        in_specs=[hbm, hbm, hbm, vmem, vmem, vmem, hbm, vmem, vmem, hbm],
        out_specs=vmem,
        scratch_shapes=[
            pltpu.VMEM((TOK, DK), BF16),
            pltpu.VMEM((TOK, DK), BF16),
            pltpu.VMEM((TOK, DV), BF16),
            pltpu.VMEM((DK, DV), F32),
            pltpu.VMEM((NS, 64, DV), BF16),
            pltpu.VMEM((NS, 64, DV), BF16),
            pltpu.VMEM((NS, 8, 128), F32),
            pltpu.VMEM((NS, 16, 256), BF16),
            pltpu.VMEM((NS, 16, 256), BF16),
            pltpu.VMEM((NS, 16, 256), BF16),
            pltpu.VMEM((NS, 16, 256), BF16),
            pltpu.VMEM((TOK, DV), F32),
            pltpu.VMEM((TOK, 1), F32),
            pltpu.VMEM((4, TOK, DV), BF16),
            pltpu.VMEM((TOK, DV), BF16),
            pltpu.VMEM((TOK, DV), BF16),
            pltpu.VMEM((NS, 8, 128), F32),
            dma((5,)), dma, dma((NS,)), dma, dma((NS,)), dma((16,)), dma, dma, dma, dma,
            dma, dma, dma, dma, dma, dma((4, NXT)), dma, dma((NXT,)),
        ],
        compiler_params=pltpu.CompilerParams(
            collective_id=0, has_side_effects=True, vmem_limit_bytes=56 * 2**20
        ),
    )(
        q, k, v, ig.reshape(8, 128), fg.reshape(8, 128), ds.reshape(8, 128),
        cmem.reshape(DK, DV), cnorm.reshape(2, 128), cmax.reshape(1, 1), w,
    )


def solution(mesh):
    placed = (
        P("seq", "head"),
        P("seq", "head"),
        P("seq", "head"),
        P("head", "seq"),
        P("head", "seq"),
        P("seq"),
        P("head", None, None),
        P("head", None),
        P("head"),
        P("seq", "head"),
    )
    return jax.shard_map(
        shards, mesh=mesh, in_specs=placed, out_specs=P("seq", "head"), check_vma=False
    )
```

```python
import jax
import jax.numpy as jnp
from jax import lax
from jax.experimental import pallas as pl
from jax.experimental.pallas import tpu as pltpu
from jax.sharding import PartitionSpec as P

DK = 256
DV = 512
TOK = 1024
NY, NZ = 4, 8
NS = NY * NZ
LOW = -1e30
MESH = pl.DeviceIdType.MESH
F32, BF16 = jnp.float32, jnp.bfloat16
QT = 256
XT = 128
NXT = TOK // XT


def lane_scan(a, op, fill, seg=None):
    lane = lax.broadcasted_iota(jnp.int32, a.shape, 1)
    for sh in (1, 2, 4, 8, 16, 32, 64):
        ok = lane >= sh
        if seg is not None:
            ok = ok & (pltpu.roll(seg, sh, 1) == seg)
        a = op(a, jnp.where(ok, pltpu.roll(a, sh, 1), fill))
    return a


def row_scan(a, op, fill, seg=None):
    row = lax.broadcasted_iota(jnp.int32, a.shape, 0)
    for sh in (1, 2, 4):
        ok = row >= sh
        if seg is not None:
            ok = ok & (pltpu.roll(seg, sh, 0) == seg)
        a = op(a, jnp.where(ok, pltpu.roll(a, sh, 0), fill))
    return a


def last_lane(a):
    return jnp.broadcast_to(a[:, 127:128], a.shape)


def before(a, fill):
    row = lax.broadcasted_iota(jnp.int32, a.shape, 0)
    return jnp.where(row >= 1, pltpu.roll(a, 1, 0), fill)


def running_sum(a):
    inside = lane_scan(a, jnp.add, 0.0)
    return inside + before(row_scan(last_lane(inside), jnp.add, 0.0), 0.0)


def running_max(a, seg):
    inside = lane_scan(a, jnp.maximum, LOW, seg)
    seg_end = last_lane(seg)
    ends = row_scan(last_lane(inside), jnp.maximum, LOW, seg_end)
    carried = jnp.where(before(seg_end, -1.0) == seg, before(ends, LOW), LOW)
    return jnp.maximum(inside, carried)


def column(cols, tile, size):
    per = size // 128
    return jnp.concatenate([cols[:, tile * per + i : tile * per + i + 1] for i in range(per)], 0)


def as_row(a, rows):
    return jnp.concatenate([a[i : i + 1, :] for i in range(rows)], 1)


def kernel(
    q_hbm, k_hbm, v_hbm, ig_hbm, fg_hbm, ds_hbm, cmem_hbm, cnorm_hbm, cmax_hbm, w_hbm,
    out_hbm,
    q_ref, k_ref, v_ref, cmem_ref, ig_ref, fg_ref, ds_ref, cnorm_ref, cmax_ref, out_ref,
    wfar, wown, stats, cpack, crecv, epack, erecv, num, den, hid, part_out, part_in, gates,
    in_sem, out_sem, row_sem, fsend, frecv, osend, orecv, oring, swap_send, ssend, srecv, srecv_rows,
    csend, crecv_sem, esend, erecv_sem, hsend, hrecv, psend, precv,
):
    me = lax.axis_index("seq")
    head = lax.axis_index("head")
    y, z = me // NZ, me % NZ
    x, core = head // 2, head % 2
    mate = 1 - core
    near = (x // 2) * 2 + (1 - x % 2)
    far = 3 - x
    home = (y // 2) == (x // 2)
    away = jnp.logical_not(home)
    opposite = ((y + 2) % NY) * NZ + z
    far_head = far * 2 + core

    def at(yy, zz):
        return ((yy + NY) % NY) * NZ + (zz + NZ) % NZ

    barrier = pltpu.get_barrier_semaphore()

    def greet(seq, hd):
        pl.semaphore_signal(
            barrier, inc=1, device_id={"seq": seq, "head": hd}, device_id_type=MESH
        )

    for d in range(1, NZ):
        greet(at(y, z + d), head)
    for d in range(1, NY):
        greet(at(y + d, z), head)
    greet(me, x * 2 + mate)
    greet(me, near * 2 + core)
    greet(me, far_head)

    @pl.when(away)
    def _():
        greet(opposite, far_head)

    loads = [
        pltpu.make_async_copy(a, b, in_sem.at[i])
        for i, (a, b) in enumerate(
            (
                (fg_hbm, fg_ref), (ds_hbm, ds_ref), (ig_hbm, ig_ref), (k_hbm, k_ref),
                (v_hbm, v_ref), (q_hbm, q_ref), (cmem_hbm, cmem_ref), (cnorm_hbm, cnorm_ref),
                (cmax_hbm, cmax_ref),
            )
        )
    ]
    for load in loads:
        load.start()

    def remote(src, dst, send, recv, seq, hd):
        return pltpu.make_async_remote_copy(
            src_ref=src, dst_ref=dst, send_sem=send, recv_sem=recv,
            device_id={"seq": seq, "head": hd}, device_id_type=MESH,
        )

    def total(ref, count, sem):
        part = ref.at[pl.ds(0, count)]
        return pltpu.make_async_copy(part, part, sem)

    for i in range(3):
        loads[i].wait()
    lf = fg_ref[...]
    lf = jnp.minimum(lf, 0.0) - jnp.log1p(jnp.exp(-jnp.abs(lf)))
    decay = running_sum(lf)
    seg = running_sum(ds_ref[...].astype(F32))
    u = ig_ref[...] - decay
    top = running_max(u, seg)
    local_max = decay + top
    end = lambda a: jnp.broadcast_to(a[7:8, 127:128], (1, 128))
    seg_end = end(seg)
    coeff = jnp.where(seg == seg_end, jnp.exp(jnp.minimum(u - end(top), 0.0)), 0.0) * (DK**-0.5)
    coeff_cols = jnp.transpose(coeff)
    top_cols = jnp.transpose(top)
    seg_cols = jnp.transpose(seg)

    loads[3].wait()
    keyed = [
        k_ref[i * 128 : (i + 1) * 128, :].astype(F32) * coeff_cols[:, i : i + 1] for i in range(8)
    ]
    normal = sum(jnp.sum(t, axis=0, keepdims=True) for t in keyed)
    stats[me, 0:1, :] = normal[:, :128]
    stats[me, 1:2, :] = normal[:, 128:]
    stats[me, 2:3, :] = end(local_max)
    stats[me, 3:4, :] = end(decay)
    stats[me, 4:5, :] = jnp.where(seg_end > 0.5, 1.0, 0.0)
    pl.semaphore_wait(barrier, jnp.where(home, 13, 14))

    mine_row = (y % 2) * NZ + z
    upper, lower = w_hbm.at[pl.ds(0, 64)], w_hbm.at[pl.ds(64, 64)]
    first, second = 2 * mine_row, 2 * mine_row + 1
    stay = pltpu.make_async_copy(upper, wown.at[first], in_sem.at[9])

    @pl.when(home)
    def _():
        stay.start()
        remote(lower, wown.at[second], swap_send, orecv.at[opposite], opposite, head).start()

    @pl.when(away)
    def _():
        remote(upper, wfar.at[first], swap_send, frecv.at[me], me, far_head).start()
        remote(lower, wfar.at[second], swap_send, frecv.at[opposite], opposite, far_head).start()

    for d in range(1, NZ):
        remote(stats.at[me], stats.at[me], ssend, srecv, at(y, z + d), head).start()

    for d in range(1, NY):
        pl.semaphore_signal(
            row_sem, inc=1, device_id={"seq": at(y + d, z), "head": head}, device_id_type=MESH
        )

    loads[4].wait()
    memory = lax.dot_general(
        jnp.concatenate([t.astype(BF16) for t in keyed], 0), v_ref[...],
        (((0,), (0,)), ((), ())), preferred_element_type=F32,
    ).astype(BF16)
    cpack[0:16] = memory[:, :256].reshape(16, 16, 256)
    cpack[16:32] = memory[:, 256:].reshape(16, 16, 256)
    crecv[me] = cpack[me]

    def place(yy, zz):
        yy = (yy + NY) % NY
        half = jnp.where((yy // 2) == (x // 2), 0, 1)
        return ((yy % 2) * NZ + (zz + NZ) % NZ) * 2 + half

    def f_copy(yy, zz, dev):
        piece = wfar.at[place(yy, zz)]
        return remote(piece, piece, fsend, frecv.at[at(yy, zz)], dev, head)

    def o_copy(yy, dev):
        piece = wown.at[place(yy, z)]
        return remote(piece, piece, osend, orecv.at[at(yy, z)], dev, head)

    def r_copy(a, zz, dev):
        row = a * NZ + (zz + NZ) % NZ
        piece = wown.at[pl.ds(row * 2, 2)]
        return remote(piece, piece, osend, oring.at[row], dev, head)

    def f_sends(yy, zz, zs, ys):
        for dz in zs:
            f_copy(yy, zz, at(y, z + dz)).start()
        for dy in ys:
            f_copy(yy, zz, at(y + dy, z)).start()

    def z_step(k):
        f_copy(y, z - k, me).wait_recv()
        f_sends(y, z - k, (1,) if k <= 3 else (), (1, -1))
        if k <= 3:
            f_copy(y, z + k, me).wait_recv()
            f_sends(y, z + k, (-1,) if k <= 2 else (), (1, -1))

    def y_step(o, up):
        f_copy(y - 1, z + o, me).wait_recv()
        f_copy(y + 1, z + o, me).wait_recv()
        if up:
            f_sends(y - 1, z + o, (), (1,))
        else:
            f_sends(y + 1, z + o, (), (-1,))

    def attend(tile):
        n = (tile + 1) * QT
        qt = q_ref[tile * QT : (tile + 1) * QT, :]
        scores = lax.dot_general(
            qt, k_ref[:n, :], (((1,), (1,)), ((), ())), preferred_element_type=F32
        )
        blocks = n // 128
        u_row, seg_row = as_row(u, blocks), as_row(seg, blocks)
        spot = lax.broadcasted_iota(jnp.int32, (QT, n), 0) + tile * QT
        allowed = (lax.broadcasted_iota(jnp.int32, (QT, n), 1) <= spot) & (
            seg_row == column(seg_cols, tile, QT)
        )
        gain = jnp.exp(u_row - column(top_cols, tile, QT))
        weights = jnp.where(allowed, gain * (DK**-0.5), 0.0) * scores
        den[tile * QT : (tile + 1) * QT, :] = jnp.sum(weights, axis=1, keepdims=True)
        num[tile * QT : (tile + 1) * QT, :] = jnp.dot(
            weights.astype(BF16), v_ref[:n, :], preferred_element_type=F32
        )

    f_copy(y, z, me).wait_recv()
    f_sends(y, z, (1, -1), (1, -1))
    pl.semaphore_wait(row_sem, NY - 1)
    for d in range(1, NS):
        dev = (me + d) % NS
        remote(cpack.at[dev], crecv.at[me], csend, crecv_sem, dev, head).start()
    loads[5].wait()
    attend(0)
    total(stats, NZ - 1, srecv).wait()
    row = stats.at[pl.ds(pl.multiple_of(y * NZ, NZ), NZ)]
    for dy in (1, 2, 3):
        remote(row, row, ssend, srecv_rows, at(y + dy, z), head).start()

    @pl.when(home)
    def _():
        stay.wait()
        remote(lower, wown.at[second], swap_send, orecv.at[opposite], opposite, head).wait_send()

    @pl.when(away)
    def _():
        pltpu.make_async_copy(w_hbm, w_hbm, swap_send).wait()
        o_copy(y, me).wait_recv()

    for dy in (1, -1):
        o_copy(y, at(y + dy, z)).start()
    z_step(1)
    attend(1)
    attend(2)
    z_step(2)
    attend(3)

    for i in (6, 7, 8):
        loads[i].wait()
    total(stats, NS - NZ, srecv_rows).wait()
    m = jnp.broadcast_to(cmax_ref[...], (1, 128))
    n0, n1 = cnorm_ref[0:1, :], cnorm_ref[1:2, :]
    em, e0, e1 = m, n0, n1
    for j in range(NS - 1):
        keep = stats[j, 4:5, :] < 0.5
        inward = m + stats[j, 3:4, :]
        later = stats[j, 2:3, :]
        m = jnp.where(keep, jnp.maximum(inward, later), later)
        old = jnp.where(keep, jnp.exp(jnp.minimum(inward - m, 0.0)), 0.0)
        new = jnp.exp(later - m)
        n0 = old * n0 + new * stats[j, 0:1, :]
        n1 = old * n1 + new * stats[j, 1:2, :]
        here = me == j + 1
        em, e0, e1 = (jnp.where(here, b, a) for a, b in ((em, m), (e0, n0), (e1, n1)))
        gates[j, 0:1, :] = old
        gates[j, 1:2, :] = new

    inward = jnp.broadcast_to(em, (8, 128)) + decay
    fresh = seg < 0.5
    merged = jnp.where(fresh, jnp.maximum(inward, local_max), local_max)
    carried = jnp.where(fresh, jnp.exp(jnp.minimum(inward - merged, 0.0)), 0.0)
    own = jnp.exp(local_max - merged)
    carried_cols, own_cols = jnp.transpose(carried), jnp.transpose(own)
    en = jnp.concatenate([e0, e1], 1)
    high = en.astype(BF16)
    rest = en - high.astype(F32)
    mid = rest.astype(BF16)
    low = (rest - mid.astype(F32)).astype(BF16)
    norms = jnp.concatenate(
        [high.astype(F32), mid.astype(F32), low.astype(F32), jnp.zeros((5, DK), F32)], 0
    ).astype(BF16)
    sden = lax.dot_general(
        q_ref[...], norms, (((1,), (1,)), ((), ())), preferred_element_type=F32
    )
    sden = jnp.sum(sden, axis=1, keepdims=True)
    for i in range(8):
        rows = slice(i * 128, (i + 1) * 128)
        o, c = own_cols[:, i : i + 1], carried_cols[:, i : i + 1]
        whole = o * den[rows, :] + c * sden[rows, :]
        inverse = 1.0 / jnp.maximum(jnp.abs(whole), 1.0)
        den[rows, :] = c * inverse
        num[rows, :] = num[rows, :] * (o * inverse)
    z_step(3)

    group, half = me % 16, me // 16
    carry_rows = cmem_ref[pl.ds(pl.multiple_of(group * 16, 16), 16), :]
    state = jnp.where(half == 0, carry_rows[:, :256], carry_rows[:, 256:])
    total(crecv, NS - 1, crecv_sem).wait()
    epack[0] = state.astype(BF16)
    for j in range(NS - 1):
        old = jnp.concatenate([gates[j, 0:1, :]] * 2, 1)
        new = jnp.concatenate([gates[j, 1:2, :]] * 2, 1)
        state = old * state + new * crecv[j].astype(F32)
        epack[j + 1] = state.astype(BF16)
    erecv[me] = epack[me]
    for d in range(1, NS):
        dev = (me + d) % NS
        remote(epack.at[dev], erecv.at[me], esend, erecv_sem, dev, head).start()

    z_step(4)
    o_copy(y - 1, me).wait_recv()
    o_copy(y + 1, me).wait_recv()
    lift = z % 2 == 0
    o_copy(jnp.where(lift, y + 3, y + 1), at(jnp.where(lift, y + 1, y + 3), z)).start()
    order = (
        (0, True), (-1, True), (1, False), (-2, False),
        (2, True), (-3, True), (3, False), (-4, False),
    )
    for o, up in order:
        y_step(o, up)

    total(erecv, NS - 1, erecv_sem).wait()
    entry_a = erecv[0:16].reshape(256, 256)
    entry_b = erecv[16:32].reshape(256, 256)
    mine, theirs = (x % 2) * 2 + core, (x % 2) * 2 + mate
    other, other_mate = (1 - x % 2) * 2 + core, (1 - x % 2) * 2 + mate

    def rows_of(t):
        return pl.ds(pl.multiple_of(t * XT, XT), XT)

    def h_copy(slot, t, hd):
        tile = hid.at[slot, rows_of(t)]
        return remote(tile, tile, hsend, hrecv.at[slot, t], me, hd)

    def make_hidden(t, c):
        rows = rows_of(t)
        qt = q_ref[rows, :]
        scale = den[rows, :]
        for part, e in ((slice(0, 256), entry_a), (slice(256, 512), entry_b)):
            got = jnp.dot(qt, e, preferred_element_type=F32)
            hid[mine, rows, part] = (num[rows, part] + scale * got).astype(BF16)
        h_copy(mine, t, near * 2 + core).start()
        h_copy(mine, t, x * 2 + mate).start()
        return c

    lax.fori_loop(0, NXT, make_hidden, 0)

    o_copy(y + 2, me).wait_recv()
    for a in (0, 1):
        for dz in (1, -1):
            r_copy(a, z, at(y, z + dz)).start()
    for o, _ in order:
        f_copy(y + 2, z + o, me).wait_recv()

    def p_copy(t):
        return remote(
            part_out.at[rows_of(t)], part_in.at[rows_of(t)], psend, precv.at[t], me, far_head
        )

    def project(t, w_ref):
        whole = None
        for j in range(4):
            w = w_ref[8 * j : 8 * j + 8].reshape(DV, DV)
            term = jnp.dot(hid[j, rows_of(t), :], w, preferred_element_type=F32)
            whole = term if whole is None else whole + term
        return whole

    def ring_step(t):
        k, a = t // 2 + 1, t % 2

        @pl.when(k <= 4 - a)
        def _():
            r_copy(a, z - k, me).wait_recv()

        @pl.when(k <= 3 - a)
        def _():
            r_copy(a, z - k, at(y, z + 1)).start()

        @pl.when(k <= 3 + a)
        def _():
            r_copy(a, z + k, me).wait_recv()

        @pl.when(k <= 2 + a)
        def _():
            r_copy(a, z + k, at(y, z - 1)).start()

    def cross(t, c):
        h_copy(other, t, head).wait_recv()
        h_copy(other, t, x * 2 + mate).start()
        h_copy(theirs, t, head).wait_recv()
        h_copy(other_mate, t, head).wait_recv()
        part_out[rows_of(t), :] = project(t, wfar).astype(BF16)
        p_copy(t).start()
        ring_step(t)
        return c

    lax.fori_loop(0, NXT, cross, 0)

    def finish(t, c):
        kept = project(t, wown)
        p_copy(t).wait_recv()
        rows = rows_of(t)
        out_ref[rows, :] = (kept + part_in[rows, :].astype(F32)).astype(BF16)
        pltpu.make_async_copy(out_ref.at[rows], out_hbm.at[rows], out_sem).start()
        return c

    lax.fori_loop(0, NXT, finish, 0)

    total(wfar, 31, fsend).wait()
    total(wown, 31, osend).wait()
    total(stats, 31, ssend).wait()
    total(cpack, 31, csend).wait()
    total(epack, 31, esend).wait()
    total(hid, 3, hsend).wait()
    pltpu.make_async_copy(part_out, part_out, psend).wait()
    pltpu.make_async_copy(out_ref, out_hbm, out_sem).wait()


def hand_on(src, dst, sem):
    parts = [
        pltpu.make_async_copy(src.at[pl.ds(i * 128, 128)], dst.at[pl.ds(i * 128, 128)], sem.at[i])
        for i in range(TOK // 128)
    ]
    for part in parts:
        part.start()
    for part in parts:
        part.wait()


def shards(q, k, v, ig, fg, ds, cmem, cnorm, cmax, w):
    dma = pltpu.SemaphoreType.DMA
    hbm = pl.BlockSpec(memory_space=pl.ANY)
    mixed = pl.pallas_call(
        kernel,
        out_shape=jax.ShapeDtypeStruct((TOK, DV), BF16),
        in_specs=[hbm] * 10,
        out_specs=hbm,
        scratch_shapes=[
            pltpu.VMEM((TOK, DK), BF16),
            pltpu.VMEM((TOK, DK), BF16),
            pltpu.VMEM((TOK, DV), BF16),
            pltpu.VMEM((DK, DV), F32),
            pltpu.VMEM((8, 128), F32),
            pltpu.VMEM((8, 128), F32),
            pltpu.VMEM((8, 128), jnp.int32),
            pltpu.VMEM((2, 128), F32),
            pltpu.VMEM((1, 1), F32),
            pltpu.VMEM((TOK, DV), BF16),
            pltpu.VMEM((NS, 64, DV), BF16),
            pltpu.VMEM((NS, 64, DV), BF16),
            pltpu.VMEM((NS, 8, 128), F32),
            pltpu.VMEM((NS, 16, 256), BF16),
            pltpu.VMEM((NS, 16, 256), BF16),
            pltpu.VMEM((NS, 16, 256), BF16),
            pltpu.VMEM((NS, 16, 256), BF16),
            pltpu.VMEM((TOK, DV), F32),
            pltpu.VMEM((TOK, 1), F32),
            pltpu.VMEM((4, TOK, DV), BF16),
            pltpu.VMEM((TOK, DV), BF16),
            pltpu.VMEM((TOK, DV), BF16),
            pltpu.VMEM((NS, 8, 128), F32),
            dma((10,)), dma, pltpu.SemaphoreType.REGULAR, dma, dma((NS,)), dma, dma((NS,)), dma((16,)), dma, dma, dma, dma,
            dma, dma, dma, dma, dma, dma((4, NXT)), dma, dma((NXT,)),
        ],
        compiler_params=pltpu.CompilerParams(
            collective_id=0, has_side_effects=True, vmem_limit_bytes=56 * 2**20
        ),
    )(
        q, k, v, ig.reshape(8, 128), fg.reshape(8, 128), ds.reshape(8, 128),
        cmem.reshape(DK, DV), cnorm.reshape(2, 128), cmax.reshape(1, 1), w,
    )
    return pl.pallas_call(
        hand_on,
        out_shape=jax.ShapeDtypeStruct((TOK, DV), BF16),
        in_specs=[hbm],
        out_specs=hbm,
        scratch_shapes=[dma((TOK // 128,))],
        compiler_params=pltpu.CompilerParams(vmem_limit_bytes=56 * 2**20),
    )(mixed)


def solution(mesh):
    placed = (
        P("seq", "head"),
        P("seq", "head"),
        P("seq", "head"),
        P("head", "seq"),
        P("head", "seq"),
        P("seq"),
        P("head", None, None),
        P("head", None),
        P("head"),
        P("seq", "head"),
    )
    return jax.shard_map(
        shards, mesh=mesh, in_specs=placed, out_specs=P("seq", "head"), check_vma=False
    )
```

```python
import jax
import jax.numpy as jnp
from jax import lax
from jax.experimental import pallas as pl
from jax.experimental.pallas import tpu as pltpu
from jax.sharding import PartitionSpec as P

DK = 256
DV = 512
TOK = 1024
NY, NZ = 4, 8
NS = NY * NZ
LOW = -1e30
MESH = pl.DeviceIdType.MESH
F32, BF16 = jnp.float32, jnp.bfloat16
QT = 256
XT = 128
NXT = TOK // XT


def lane_scan(a, op, fill, seg=None):
    lane = lax.broadcasted_iota(jnp.int32, a.shape, 1)
    for sh in (1, 2, 4, 8, 16, 32, 64):
        ok = lane >= sh
        if seg is not None:
            ok = ok & (pltpu.roll(seg, sh, 1) == seg)
        a = op(a, jnp.where(ok, pltpu.roll(a, sh, 1), fill))
    return a


def row_scan(a, op, fill, seg=None):
    row = lax.broadcasted_iota(jnp.int32, a.shape, 0)
    for sh in (1, 2, 4):
        ok = row >= sh
        if seg is not None:
            ok = ok & (pltpu.roll(seg, sh, 0) == seg)
        a = op(a, jnp.where(ok, pltpu.roll(a, sh, 0), fill))
    return a


def last_lane(a):
    return jnp.broadcast_to(a[:, 127:128], a.shape)


def before(a, fill):
    row = lax.broadcasted_iota(jnp.int32, a.shape, 0)
    return jnp.where(row >= 1, pltpu.roll(a, 1, 0), fill)


def running_sum(a):
    inside = lane_scan(a, jnp.add, 0.0)
    return inside + before(row_scan(last_lane(inside), jnp.add, 0.0), 0.0)


def running_max(a, seg):
    inside = lane_scan(a, jnp.maximum, LOW, seg)
    seg_end = last_lane(seg)
    ends = row_scan(last_lane(inside), jnp.maximum, LOW, seg_end)
    carried = jnp.where(before(seg_end, -1.0) == seg, before(ends, LOW), LOW)
    return jnp.maximum(inside, carried)


def column(cols, tile, size):
    per = size // 128
    return jnp.concatenate([cols[:, tile * per + i : tile * per + i + 1] for i in range(per)], 0)


def as_row(a, rows):
    return jnp.concatenate([a[i : i + 1, :] for i in range(rows)], 1)


def kernel(
    q_hbm, k_hbm, v_hbm, ig_hbm, fg_hbm, ds_hbm, cmem_hbm, cnorm_hbm, cmax_hbm, w_hbm,
    out_ref,
    q_ref, k_ref, v_ref, cmem_ref, ig_ref, fg_ref, ds_ref, cnorm_ref, cmax_ref,
    wfar, wown, stats, rowstats, cpack, crecv, tpack, trecv, epack, erecv, num, den, hid, part_out, part_in, gates,
    in_sem, fsend, frecv, osend, orecv, oring, swap_send, ssend, srecv, srecv_rows,
    csend, crecv_sem, tsend, trecv_sem, esend, erecv_sem, hsend, hrecv, psend, precv,
):
    me = lax.axis_index("seq")
    head = lax.axis_index("head")
    y, z = me // NZ, me % NZ
    x, core = head // 2, head % 2
    mate = 1 - core
    near = (x // 2) * 2 + (1 - x % 2)
    far = 3 - x
    home = (y // 2) == (x // 2)
    away = jnp.logical_not(home)
    opposite = ((y + 2) % NY) * NZ + z
    far_head = far * 2 + core

    def at(yy, zz):
        return ((yy + NY) % NY) * NZ + (zz + NZ) % NZ

    barrier = pltpu.get_barrier_semaphore()

    def greet(seq, hd):
        pl.semaphore_signal(
            barrier, inc=1, device_id={"seq": seq, "head": hd}, device_id_type=MESH
        )

    for d in range(1, NZ):
        greet(at(y, z + d), head)
    for d in range(1, NY):
        greet(at(y + d, z), head)
    greet(me, x * 2 + mate)
    greet(me, near * 2 + core)
    greet(me, far_head)

    @pl.when(away)
    def _():
        greet(opposite, far_head)

    loads = [
        pltpu.make_async_copy(a, b, in_sem.at[i])
        for i, (a, b) in enumerate(
            (
                (fg_hbm, fg_ref), (ds_hbm, ds_ref), (ig_hbm, ig_ref), (k_hbm, k_ref),
                (v_hbm, v_ref), (q_hbm, q_ref), (cmem_hbm, cmem_ref), (cnorm_hbm, cnorm_ref),
                (cmax_hbm, cmax_ref),
            )
        )
    ]
    for load in loads:
        load.start()

    def remote(src, dst, send, recv, seq, hd):
        return pltpu.make_async_remote_copy(
            src_ref=src, dst_ref=dst, send_sem=send, recv_sem=recv,
            device_id={"seq": seq, "head": hd}, device_id_type=MESH,
        )

    def total(ref, count, sem):
        part = ref.at[pl.ds(0, count)]
        return pltpu.make_async_copy(part, part, sem)

    for i in range(3):
        loads[i].wait()
    lf = fg_ref[...]
    lf = jnp.minimum(lf, 0.0) - jnp.log1p(jnp.exp(-jnp.abs(lf)))
    decay = running_sum(lf)
    seg = running_sum(ds_ref[...].astype(F32))
    u = ig_ref[...] - decay
    top = running_max(u, seg)
    local_max = decay + top
    end = lambda a: jnp.broadcast_to(a[7:8, 127:128], (1, 128))
    seg_end = end(seg)
    coeff = jnp.where(seg == seg_end, jnp.exp(jnp.minimum(u - end(top), 0.0)), 0.0) * (DK**-0.5)
    coeff_cols = jnp.transpose(coeff)
    top_cols = jnp.transpose(top)
    seg_cols = jnp.transpose(seg)

    loads[3].wait()
    keyed = [
        k_ref[i * 128 : (i + 1) * 128, :].astype(F32) * coeff_cols[:, i : i + 1] for i in range(8)
    ]
    normal = sum(jnp.sum(t, axis=0, keepdims=True) for t in keyed)
    stats[me, 0:1, :] = normal[:, :128]
    stats[me, 1:2, :] = normal[:, 128:]
    stats[me, 2:3, :] = end(local_max)
    stats[me, 3:4, :] = end(decay)
    stats[me, 4:5, :] = jnp.where(seg_end > 0.5, 1.0, 0.0)
    pl.semaphore_wait(barrier, jnp.where(home, 13, 14))

    mine_row = (y % 2) * NZ + z
    upper, lower = w_hbm.at[pl.ds(0, 64)], w_hbm.at[pl.ds(64, 64)]
    first, second = 2 * mine_row, 2 * mine_row + 1
    stay = pltpu.make_async_copy(upper, wown.at[first], in_sem.at[9])

    @pl.when(home)
    def _():
        stay.start()
        remote(lower, wown.at[second], swap_send, orecv.at[opposite], opposite, head).start()

    @pl.when(away)
    def _():
        remote(upper, wfar.at[first], swap_send, frecv.at[me], me, far_head).start()
        remote(lower, wfar.at[second], swap_send, frecv.at[opposite], opposite, far_head).start()

    for d in range(1, NZ):
        remote(stats.at[me], stats.at[me], ssend, srecv, at(y, z + d), head).start()

    loads[4].wait()
    memory = lax.dot_general(
        jnp.concatenate([t.astype(BF16) for t in keyed], 0), v_ref[...],
        (((0,), (0,)), ((), ())), preferred_element_type=F32,
    ).astype(BF16)
    cpack[...] = memory.reshape(NZ, DK // NZ, DV)
    crecv[z] = cpack[z]
    for d in range(1, NZ):
        to = (z + d) % NZ
        remote(cpack.at[to], crecv.at[z], csend, crecv_sem, at(y, to), head).start()

    def place(yy, zz):
        yy = (yy + NY) % NY
        half = jnp.where((yy // 2) == (x // 2), 0, 1)
        return ((yy % 2) * NZ + (zz + NZ) % NZ) * 2 + half

    def f_copy(yy, zz, dev):
        piece = wfar.at[place(yy, zz)]
        return remote(piece, piece, fsend, frecv.at[at(yy, zz)], dev, head)

    def o_copy(yy, dev):
        piece = wown.at[place(yy, z)]
        return remote(piece, piece, osend, orecv.at[at(yy, z)], dev, head)

    def r_copy(a, zz, dev):
        row = a * NZ + (zz + NZ) % NZ
        piece = wown.at[pl.ds(row * 2, 2)]
        return remote(piece, piece, osend, oring.at[row], dev, head)

    def f_sends(yy, zz, zs, ys):
        for dz in zs:
            f_copy(yy, zz, at(y, z + dz)).start()
        for dy in ys:
            f_copy(yy, zz, at(y + dy, z)).start()

    def z_step(k):
        f_copy(y, z - k, me).wait_recv()
        f_sends(y, z - k, (1,) if k <= 3 else (), (1, -1))
        if k <= 3:
            f_copy(y, z + k, me).wait_recv()
            f_sends(y, z + k, (-1,) if k <= 2 else (), (1, -1))

    def y_step(o, up):
        f_copy(y - 1, z + o, me).wait_recv()
        f_copy(y + 1, z + o, me).wait_recv()
        if up:
            f_sends(y - 1, z + o, (), (1,))
        else:
            f_sends(y + 1, z + o, (), (-1,))

    def attend(tile):
        n = (tile + 1) * QT
        qt = q_ref[tile * QT : (tile + 1) * QT, :]
        scores = lax.dot_general(
            qt, k_ref[:n, :], (((1,), (1,)), ((), ())), preferred_element_type=F32
        )
        blocks = n // 128
        u_row, seg_row = as_row(u, blocks), as_row(seg, blocks)
        spot = lax.broadcasted_iota(jnp.int32, (QT, n), 0) + tile * QT
        allowed = (lax.broadcasted_iota(jnp.int32, (QT, n), 1) <= spot) & (
            seg_row == column(seg_cols, tile, QT)
        )
        gain = jnp.exp(u_row - column(top_cols, tile, QT))
        weights = jnp.where(allowed, gain * (DK**-0.5), 0.0) * scores
        den[tile * QT : (tile + 1) * QT, :] = jnp.sum(weights, axis=1, keepdims=True)
        num[tile * QT : (tile + 1) * QT, :] = jnp.dot(
            weights.astype(BF16), v_ref[:n, :], preferred_element_type=F32
        )

    f_copy(y, z, me).wait_recv()
    f_sends(y, z, (1, -1), (1, -1))
    loads[5].wait()
    attend(0)
    total(stats, NZ - 1, srecv).wait()
    base = y * NZ
    m = jnp.full((1, 128), LOW, F32)
    g = r = n0 = n1 = jnp.zeros((1, 128), F32)
    prefixes = []
    for k in range(NZ):
        prefixes.append((m, g, r, n0, n1))
        m2, g2, r2 = (stats[base + k, c : c + 1, :] for c in (2, 3, 4))
        inward = m + g2
        m = jnp.where(r2 < 0.5, jnp.maximum(inward, m2), m2)
        old = jnp.where(r2 < 0.5, jnp.exp(jnp.minimum(inward - m, 0.0)), 0.0)
        new = jnp.exp(m2 - m)
        n0 = old * n0 + new * stats[base + k, 0:1, :]
        n1 = old * n1 + new * stats[base + k, 1:2, :]
        g, r = g + g2, jnp.maximum(r, r2)
        gates[k, 0:1, :] = old
        gates[k, 1:2, :] = new
    for c, value in enumerate((n0, n1, m, g, r)):
        rowstats[y, c : c + 1, :] = value
    for dy in (1, 2, 3):
        remote(
            rowstats.at[y], rowstats.at[y], ssend, srecv_rows, at(y + dy, z), head
        ).start()

    @pl.when(home)
    def _():
        stay.wait()
        remote(lower, wown.at[second], swap_send, orecv.at[opposite], opposite, head).wait_send()

    @pl.when(away)
    def _():
        pltpu.make_async_copy(w_hbm, w_hbm, swap_send).wait()
        o_copy(y, me).wait_recv()

    for dy in (1, -1):
        o_copy(y, at(y + dy, z)).start()
    z_step(1)
    attend(1)
    y_step(0, True)
    attend(2)
    z_step(2)
    attend(3)

    for i in (6, 7, 8):
        loads[i].wait()
    total(rowstats, NY - 1, srecv_rows).wait()
    m = jnp.broadcast_to(cmax_ref[...], (1, 128))
    n0, n1 = cnorm_ref[0:1, :], cnorm_ref[1:2, :]
    for row_at in range(NY - 1):
        m2, g2, r2 = (rowstats[row_at, c : c + 1, :] for c in (2, 3, 4))
        inward = m + g2
        after = jnp.where(r2 < 0.5, jnp.maximum(inward, m2), m2)
        old = jnp.where(r2 < 0.5, jnp.exp(jnp.minimum(inward - after, 0.0)), 0.0)
        new = jnp.exp(m2 - after)
        earlier = row_at < y
        n0 = jnp.where(earlier, old * n0 + new * rowstats[row_at, 0:1, :], n0)
        n1 = jnp.where(earlier, old * n1 + new * rowstats[row_at, 1:2, :], n1)
        m = jnp.where(earlier, after, m)
        gates[NZ + row_at, 0:1, :] = old
        gates[NZ + row_at, 1:2, :] = new
    em, e0, e1 = m, n0, n1
    for k in range(NZ):
        m2, g2, r2, p0, p1 = prefixes[k]
        inward = m + g2
        after = jnp.where(r2 < 0.5, jnp.maximum(inward, m2), m2)
        old = jnp.where(r2 < 0.5, jnp.exp(jnp.minimum(inward - after, 0.0)), 0.0)
        new = jnp.exp(m2 - after)
        here = z == k
        em = jnp.where(here, after, em)
        e0 = jnp.where(here, old * n0 + new * p0, e0)
        e1 = jnp.where(here, old * n1 + new * p1, e1)
        gates[NZ + NY + k, 0:1, :] = old
        gates[NZ + NY + k, 1:2, :] = new

    inward = jnp.broadcast_to(em, (8, 128)) + decay
    fresh = seg < 0.5
    merged = jnp.where(fresh, jnp.maximum(inward, local_max), local_max)
    carried = jnp.where(fresh, jnp.exp(jnp.minimum(inward - merged, 0.0)), 0.0)
    own = jnp.exp(local_max - merged)
    carried_cols, own_cols = jnp.transpose(carried), jnp.transpose(own)
    en = jnp.concatenate([e0, e1], 1)
    high = en.astype(BF16)
    rest = en - high.astype(F32)
    mid = rest.astype(BF16)
    low = (rest - mid.astype(F32)).astype(BF16)
    norms = jnp.concatenate(
        [high.astype(F32), mid.astype(F32), low.astype(F32), jnp.zeros((5, DK), F32)], 0
    ).astype(BF16)
    sden = lax.dot_general(
        q_ref[...], norms, (((1,), (1,)), ((), ())), preferred_element_type=F32
    )
    sden = jnp.sum(sden, axis=1, keepdims=True)
    for i in range(8):
        rows = slice(i * 128, (i + 1) * 128)
        o, c = own_cols[:, i : i + 1], carried_cols[:, i : i + 1]
        whole = o * den[rows, :] + c * sden[rows, :]
        inverse = 1.0 / jnp.maximum(jnp.abs(whole), 1.0)
        den[rows, :] = c * inverse
        num[rows, :] = num[rows, :] * (o * inverse)

    def factor(j, kind):
        return jnp.concatenate([gates[j, kind : kind + 1, :]] * (DV // 128), 1)

    total(crecv, NZ - 1, crecv_sem).wait()
    part = jnp.zeros((DK // NZ, DV), F32)
    parts = []
    for k in range(NZ):
        parts.append(part)
        part = factor(k, 0) * part + factor(k, 1) * crecv[k].astype(F32)
    tpack[...] = part.astype(BF16)
    for dy in (1, 2, 3):
        remote(tpack, trecv.at[y], tsend, trecv_sem, at(y + dy, z), head).start()
    z_step(3)
    y_step(-1, True)
    y_step(1, False)

    state = cmem_ref[pl.ds(pl.multiple_of(z * (DK // NZ), DK // NZ), DK // NZ), :]
    total(trecv, NY - 1, trecv_sem).wait()
    for row_at in range(NY - 1):
        joined = factor(NZ + row_at, 0) * state + factor(NZ + row_at, 1) * trecv[row_at].astype(F32)
        state = jnp.where(row_at < y, joined, state)
    for k in range(NZ):
        at_k = NZ + NY + k
        epack[k] = (factor(at_k, 0) * state + factor(at_k, 1) * parts[k]).astype(BF16)
    erecv[z] = epack[z]
    for d in range(1, NZ):
        to = (z + d) % NZ
        remote(epack.at[to], erecv.at[z], esend, erecv_sem, at(y, to), head).start()

    z_step(4)
    o_copy(y - 1, me).wait_recv()
    o_copy(y + 1, me).wait_recv()
    lift = z % 2 == 0
    o_copy(jnp.where(lift, y + 3, y + 1), at(jnp.where(lift, y + 1, y + 3), z)).start()

    y_step(-2, False)
    y_step(2, True)
    total(erecv, NZ - 1, erecv_sem).wait()
    entry = erecv[...].reshape(DK, DV)
    mine, theirs = (x % 2) * 2 + core, (x % 2) * 2 + mate
    other, other_mate = (1 - x % 2) * 2 + core, (1 - x % 2) * 2 + mate

    def rows_of(t):
        return pl.ds(pl.multiple_of(t * XT, XT), XT)

    def h_copy(slot, t, hd):
        tile = hid.at[slot, rows_of(t)]
        return remote(tile, tile, hsend, hrecv.at[slot, t], me, hd)

    def make_hidden(t, c):
        rows = rows_of(t)
        qt = q_ref[rows, :]
        scale = den[rows, :]
        got = jnp.dot(qt, entry, preferred_element_type=F32)
        hid[mine, rows, :] = (num[rows, :] + scale * got).astype(BF16)
        h_copy(mine, t, near * 2 + core).start()
        h_copy(mine, t, x * 2 + mate).start()
        return c

    lax.fori_loop(0, NXT, make_hidden, 0)

    y_step(-3, True)
    y_step(3, False)
    y_step(-4, False)
    o_copy(y + 2, me).wait_recv()
    for a in (0, 1):
        for dz in (1, -1):
            r_copy(a, z, at(y, z + dz)).start()
    for o in range(-4, 4):
        f_copy(y + 2, z + o, me).wait_recv()

    def p_copy(t):
        return remote(
            part_out.at[rows_of(t)], part_in.at[rows_of(t)], psend, precv.at[t], me, far_head
        )

    def project(t, w_ref):
        whole = None
        for j in range(4):
            w = w_ref[8 * j : 8 * j + 8].reshape(DV, DV)
            term = jnp.dot(hid[j, rows_of(t), :], w, preferred_element_type=F32)
            whole = term if whole is None else whole + term
        return whole

    def ring_step(t):
        k, a = t // 2 + 1, t % 2

        @pl.when(k <= 4 - a)
        def _():
            r_copy(a, z - k, me).wait_recv()

        @pl.when(k <= 3 - a)
        def _():
            r_copy(a, z - k, at(y, z + 1)).start()

        @pl.when(k <= 3 + a)
        def _():
            r_copy(a, z + k, me).wait_recv()

        @pl.when(k <= 2 + a)
        def _():
            r_copy(a, z + k, at(y, z - 1)).start()

    def cross(t, c):
        h_copy(other, t, head).wait_recv()
        h_copy(other, t, x * 2 + mate).start()
        h_copy(theirs, t, head).wait_recv()
        h_copy(other_mate, t, head).wait_recv()
        part_out[rows_of(t), :] = project(t, wfar).astype(BF16)
        p_copy(t).start()
        ring_step(t)
        return c

    lax.fori_loop(0, NXT, cross, 0)

    def finish(t, c):
        kept = project(t, wown)
        p_copy(t).wait_recv()
        rows = rows_of(t)
        out_ref[rows, :] = (kept + part_in[rows, :].astype(F32)).astype(BF16)
        return c

    lax.fori_loop(0, NXT, finish, 0)

    total(wfar, 31, fsend).wait()
    total(wown, 31, osend).wait()
    total(stats, NZ - 1 + NY - 1, ssend).wait()
    total(cpack, NZ - 1, csend).wait()
    total(trecv, NY - 1, tsend).wait()
    total(epack, NZ - 1, esend).wait()
    total(hid, 3, hsend).wait()
    pltpu.make_async_copy(part_out, part_out, psend).wait()


def shards(q, k, v, ig, fg, ds, cmem, cnorm, cmax, w):
    dma = pltpu.SemaphoreType.DMA
    hbm = pl.BlockSpec(memory_space=pl.ANY)
    return pl.pallas_call(
        kernel,
        out_shape=pltpu.VMEM((TOK, DV), BF16),
        in_specs=[hbm] * 10,
        out_specs=pl.BlockSpec(memory_space=pltpu.VMEM),
        scratch_shapes=[
            pltpu.VMEM((TOK, DK), BF16),
            pltpu.VMEM((TOK, DK), BF16),
            pltpu.VMEM((TOK, DV), BF16),
            pltpu.VMEM((DK, DV), F32),
            pltpu.VMEM((8, 128), F32),
            pltpu.VMEM((8, 128), F32),
            pltpu.VMEM((8, 128), jnp.int32),
            pltpu.VMEM((2, 128), F32),
            pltpu.VMEM((1, 1), F32),
            pltpu.VMEM((NS, 64, DV), BF16),
            pltpu.VMEM((NS, 64, DV), BF16),
            pltpu.VMEM((NS, 8, 128), F32),
            pltpu.VMEM((NY, 8, 128), F32),
            pltpu.VMEM((NZ, DK // NZ, DV), BF16),
            pltpu.VMEM((NZ, DK // NZ, DV), BF16),
            pltpu.VMEM((DK // NZ, DV), BF16),
            pltpu.VMEM((NY, DK // NZ, DV), BF16),
            pltpu.VMEM((NZ, DK // NZ, DV), BF16),
            pltpu.VMEM((NZ, DK // NZ, DV), BF16),
            pltpu.VMEM((TOK, DV), F32),
            pltpu.VMEM((TOK, 1), F32),
            pltpu.VMEM((4, TOK, DV), BF16),
            pltpu.VMEM((TOK, DV), BF16),
            pltpu.VMEM((TOK, DV), BF16),
            pltpu.VMEM((NS, 8, 128), F32),
            dma((10,)), dma, dma((NS,)), dma, dma((NS,)), dma((16,)), dma, dma, dma, dma,
            dma, dma, dma, dma, dma, dma, dma, dma((4, NXT)), dma, dma((NXT,)),
        ],
        compiler_params=pltpu.CompilerParams(
            collective_id=0, has_side_effects=True, vmem_limit_bytes=60 * 2**20
        ),
    )(
        q, k, v, ig.reshape(8, 128), fg.reshape(8, 128), ds.reshape(8, 128),
        cmem.reshape(DK, DV), cnorm.reshape(2, 128), cmax.reshape(1, 1), w,
    )


def solution(mesh):
    placed = (
        P("seq", "head"),
        P("seq", "head"),
        P("seq", "head"),
        P("head", "seq"),
        P("head", "seq"),
        P("seq"),
        P("head", None, None),
        P("head", None),
        P("head"),
        P("seq", "head"),
    )
    return jax.shard_map(
        shards, mesh=mesh, in_specs=placed, out_specs=P("seq", "head"), check_vma=False
    )
```

```python
import jax
import jax.numpy as jnp
from jax import lax
from jax.experimental import pallas as pl
from jax.experimental.pallas import tpu as pltpu
from jax.sharding import PartitionSpec as P

DK = 256
DV = 512
TOK = 1024
NY, NZ = 4, 8
NS = NY * NZ
LOW = -1e30
MESH = pl.DeviceIdType.MESH
F32, BF16 = jnp.float32, jnp.bfloat16
QT = 256
XT = 128
NXT = TOK // XT


def lane_scan(a, op, fill, seg=None):
    lane = lax.broadcasted_iota(jnp.int32, a.shape, 1)
    for sh in (1, 2, 4, 8, 16, 32, 64):
        ok = lane >= sh
        if seg is not None:
            ok = ok & (pltpu.roll(seg, sh, 1) == seg)
        a = op(a, jnp.where(ok, pltpu.roll(a, sh, 1), fill))
    return a


def row_scan(a, op, fill, seg=None):
    row = lax.broadcasted_iota(jnp.int32, a.shape, 0)
    for sh in (1, 2, 4):
        ok = row >= sh
        if seg is not None:
            ok = ok & (pltpu.roll(seg, sh, 0) == seg)
        a = op(a, jnp.where(ok, pltpu.roll(a, sh, 0), fill))
    return a


def last_lane(a):
    return jnp.broadcast_to(a[:, 127:128], a.shape)


def before(a, fill):
    row = lax.broadcasted_iota(jnp.int32, a.shape, 0)
    return jnp.where(row >= 1, pltpu.roll(a, 1, 0), fill)


def running_sum(a):
    inside = lane_scan(a, jnp.add, 0.0)
    return inside + before(row_scan(last_lane(inside), jnp.add, 0.0), 0.0)


def running_max(a, seg):
    inside = lane_scan(a, jnp.maximum, LOW, seg)
    seg_end = last_lane(seg)
    ends = row_scan(last_lane(inside), jnp.maximum, LOW, seg_end)
    carried = jnp.where(before(seg_end, -1.0) == seg, before(ends, LOW), LOW)
    return jnp.maximum(inside, carried)


def column(cols, tile, size):
    per = size // 128
    return jnp.concatenate([cols[:, tile * per + i : tile * per + i + 1] for i in range(per)], 0)


def as_row(a, rows):
    return jnp.concatenate([a[i : i + 1, :] for i in range(rows)], 1)


def kernel(
    q_hbm, k_hbm, v_hbm, ig_hbm, fg_hbm, ds_hbm, cmem_hbm, cnorm_hbm, cmax_hbm, w_hbm,
    out_ref,
    q_ref, k_ref, v_ref, cmem_ref, ig_ref, fg_ref, ds_ref, cnorm_ref, cmax_ref,
    wfar, wown, stats, rowstats, cpack, crecv, tpack, trecv, epack, erecv, num, den, hid, part_out, part_in, gates,
    in_sem, fsend, frecv, osend, orecv, oring, swap_send, ssend, srecv, srecv_rows,
    csend, crecv_sem, tsend, trecv_sem, esend, erecv_sem, hsend, hrecv, psend, precv,
):
    me = lax.axis_index("seq")
    head = lax.axis_index("head")
    y, z = me // NZ, me % NZ
    x, core = head // 2, head % 2
    mate = 1 - core
    near = (x // 2) * 2 + (1 - x % 2)
    far = 3 - x
    home = (y // 2) == (x // 2)
    away = jnp.logical_not(home)
    opposite = ((y + 2) % NY) * NZ + z
    far_head = far * 2 + core

    def at(yy, zz):
        return ((yy + NY) % NY) * NZ + (zz + NZ) % NZ

    barrier = pltpu.get_barrier_semaphore()

    def greet(seq, hd):
        pl.semaphore_signal(
            barrier, inc=1, device_id={"seq": seq, "head": hd}, device_id_type=MESH
        )

    for d in range(1, NZ):
        greet(at(y, z + d), head)
    for d in range(1, NY):
        greet(at(y + d, z), head)
    greet(me, x * 2 + mate)
    greet(me, near * 2 + core)
    greet(me, far_head)

    @pl.when(away)
    def _():
        greet(opposite, far_head)

    loads = [
        pltpu.make_async_copy(a, b, in_sem.at[i])
        for i, (a, b) in enumerate(
            (
                (fg_hbm, fg_ref), (ds_hbm, ds_ref), (ig_hbm, ig_ref), (k_hbm, k_ref),
                (v_hbm, v_ref), (q_hbm, q_ref), (cmem_hbm, cmem_ref), (cnorm_hbm, cnorm_ref),
                (cmax_hbm, cmax_ref),
            )
        )
    ]
    for load in loads:
        load.start()

    def remote(src, dst, send, recv, seq, hd):
        return pltpu.make_async_remote_copy(
            src_ref=src, dst_ref=dst, send_sem=send, recv_sem=recv,
            device_id={"seq": seq, "head": hd}, device_id_type=MESH,
        )

    def total(ref, count, sem):
        part = ref.at[pl.ds(0, count)]
        return pltpu.make_async_copy(part, part, sem)

    for i in range(3):
        loads[i].wait()
    lf = fg_ref[...]
    lf = jnp.minimum(lf, 0.0) - jnp.log1p(jnp.exp(-jnp.abs(lf)))
    decay = running_sum(lf)
    seg = running_sum(ds_ref[...].astype(F32))
    u = ig_ref[...] - decay
    top = running_max(u, seg)
    local_max = decay + top
    end = lambda a: jnp.broadcast_to(a[7:8, 127:128], (1, 128))
    seg_end = end(seg)
    coeff = jnp.where(seg == seg_end, jnp.exp(jnp.minimum(u - end(top), 0.0)), 0.0) * (DK**-0.5)
    coeff_cols = jnp.transpose(coeff)
    top_cols = jnp.transpose(top)
    seg_cols = jnp.transpose(seg)

    loads[3].wait()
    keyed = [
        k_ref[i * 128 : (i + 1) * 128, :].astype(F32) * coeff_cols[:, i : i + 1] for i in range(8)
    ]
    normal = sum(jnp.sum(t, axis=0, keepdims=True) for t in keyed)
    stats[me, 0:1, :] = normal[:, :128]
    stats[me, 1:2, :] = normal[:, 128:]
    stats[me, 2:3, :] = end(local_max)
    stats[me, 3:4, :] = end(decay)
    stats[me, 4:5, :] = jnp.where(seg_end > 0.5, 1.0, 0.0)
    pl.semaphore_wait(barrier, jnp.where(home, 13, 14))

    mine_row = (y % 2) * NZ + z
    upper, lower = w_hbm.at[pl.ds(0, 64)], w_hbm.at[pl.ds(64, 64)]
    first, second = 2 * mine_row, 2 * mine_row + 1
    stay = pltpu.make_async_copy(upper, wown.at[first], in_sem.at[9])

    @pl.when(home)
    def _():
        stay.start()
        remote(lower, wown.at[second], swap_send, orecv.at[opposite], opposite, head).start()

    @pl.when(away)
    def _():
        remote(upper, wfar.at[first], swap_send, frecv.at[me], me, far_head).start()
        remote(lower, wfar.at[second], swap_send, frecv.at[opposite], opposite, far_head).start()

    for d in range(1, NZ):
        remote(stats.at[me], stats.at[me], ssend, srecv, at(y, z + d), head).start()

    loads[4].wait()
    memory = lax.dot_general(
        jnp.concatenate([t.astype(BF16) for t in keyed], 0), v_ref[...],
        (((0,), (0,)), ((), ())), preferred_element_type=F32,
    ).astype(BF16)
    cpack[...] = memory.reshape(NZ, DK // NZ, DV)
    crecv[z] = cpack[z]
    for d in range(1, NZ):
        to = (z + d) % NZ
        remote(cpack.at[to], crecv.at[z], csend, crecv_sem, at(y, to), head).start()

    def place(yy, zz):
        yy = (yy + NY) % NY
        half = jnp.where((yy // 2) == (x // 2), 0, 1)
        return ((yy % 2) * NZ + (zz + NZ) % NZ) * 2 + half

    def f_copy(yy, zz, dev):
        piece = wfar.at[place(yy, zz)]
        return remote(piece, piece, fsend, frecv.at[at(yy, zz)], dev, head)

    def o_copy(yy, dev):
        piece = wown.at[place(yy, z)]
        return remote(piece, piece, osend, orecv.at[at(yy, z)], dev, head)

    def r_copy(a, zz, dev):
        row = a * NZ + (zz + NZ) % NZ
        piece = wown.at[pl.ds(row * 2, 2)]
        return remote(piece, piece, osend, oring.at[row], dev, head)

    def f_sends(yy, zz, zs, ys):
        for dz in zs:
            f_copy(yy, zz, at(y, z + dz)).start()
        for dy in ys:
            f_copy(yy, zz, at(y + dy, z)).start()

    def z_step(k, ys=(1, -1)):
        f_copy(y, z - k, me).wait_recv()
        f_sends(y, z - k, (1,) if k <= 3 else (), ys)
        if k <= 3:
            f_copy(y, z + k, me).wait_recv()
            f_sends(y, z + k, (-1,) if k <= 2 else (), ys)

    def y_step(o, up):
        f_copy(y - 1, z + o, me).wait_recv()
        f_copy(y + 1, z + o, me).wait_recv()
        if up:
            f_sends(y - 1, z + o, (), (1,))
        else:
            f_sends(y + 1, z + o, (), (-1,))

    def attend(tile):
        n = (tile + 1) * QT
        qt = q_ref[tile * QT : (tile + 1) * QT, :]
        scores = lax.dot_general(
            qt, k_ref[:n, :], (((1,), (1,)), ((), ())), preferred_element_type=F32
        )
        blocks = n // 128
        u_row, seg_row = as_row(u, blocks), as_row(seg, blocks)
        spot = lax.broadcasted_iota(jnp.int32, (QT, n), 0) + tile * QT
        allowed = (lax.broadcasted_iota(jnp.int32, (QT, n), 1) <= spot) & (
            seg_row == column(seg_cols, tile, QT)
        )
        gain = jnp.exp(u_row - column(top_cols, tile, QT))
        weights = jnp.where(allowed, gain * (DK**-0.5), 0.0) * scores
        den[tile * QT : (tile + 1) * QT, :] = jnp.sum(weights, axis=1, keepdims=True)
        num[tile * QT : (tile + 1) * QT, :] = jnp.dot(
            weights.astype(BF16), v_ref[:n, :], preferred_element_type=F32
        )

    f_copy(y, z, me).wait_recv()
    f_sends(y, z, (1, -1), (1, -1))
    loads[5].wait()
    attend(0)
    total(stats, NZ - 1, srecv).wait()
    base = y * NZ
    m = jnp.full((1, 128), LOW, F32)
    g = r = n0 = n1 = jnp.zeros((1, 128), F32)
    prefixes = []
    for k in range(NZ):
        prefixes.append((m, g, r, n0, n1))
        m2, g2, r2 = (stats[base + k, c : c + 1, :] for c in (2, 3, 4))
        inward = m + g2
        m = jnp.where(r2 < 0.5, jnp.maximum(inward, m2), m2)
        old = jnp.where(r2 < 0.5, jnp.exp(jnp.minimum(inward - m, 0.0)), 0.0)
        new = jnp.exp(m2 - m)
        n0 = old * n0 + new * stats[base + k, 0:1, :]
        n1 = old * n1 + new * stats[base + k, 1:2, :]
        g, r = g + g2, jnp.maximum(r, r2)
        gates[k, 0:1, :] = old
        gates[k, 1:2, :] = new
    for c, value in enumerate((n0, n1, m, g, r)):
        rowstats[y, c : c + 1, :] = value
    for dy in (1, 2, 3):
        remote(
            rowstats.at[y], rowstats.at[y], ssend, srecv_rows, at(y + dy, z), head
        ).start()

    @pl.when(home)
    def _():
        stay.wait()
        remote(lower, wown.at[second], swap_send, orecv.at[opposite], opposite, head).wait_send()

    @pl.when(away)
    def _():
        pltpu.make_async_copy(w_hbm, w_hbm, swap_send).wait()
        o_copy(y, me).wait_recv()

    for dy in (1, -1):
        o_copy(y, at(y + dy, z)).start()
    z_step(1)
    attend(1)
    y_step(0, True)
    attend(2)
    z_step(2, ())
    attend(3)

    for i in (6, 7, 8):
        loads[i].wait()
    total(rowstats, NY - 1, srecv_rows).wait()
    m = jnp.broadcast_to(cmax_ref[...], (1, 128))
    n0, n1 = cnorm_ref[0:1, :], cnorm_ref[1:2, :]
    for row_at in range(NY - 1):
        m2, g2, r2 = (rowstats[row_at, c : c + 1, :] for c in (2, 3, 4))
        inward = m + g2
        after = jnp.where(r2 < 0.5, jnp.maximum(inward, m2), m2)
        old = jnp.where(r2 < 0.5, jnp.exp(jnp.minimum(inward - after, 0.0)), 0.0)
        new = jnp.exp(m2 - after)
        earlier = row_at < y
        n0 = jnp.where(earlier, old * n0 + new * rowstats[row_at, 0:1, :], n0)
        n1 = jnp.where(earlier, old * n1 + new * rowstats[row_at, 1:2, :], n1)
        m = jnp.where(earlier, after, m)
        gates[NZ + row_at, 0:1, :] = old
        gates[NZ + row_at, 1:2, :] = new
    em, e0, e1 = m, n0, n1
    for k in range(NZ):
        m2, g2, r2, p0, p1 = prefixes[k]
        inward = m + g2
        after = jnp.where(r2 < 0.5, jnp.maximum(inward, m2), m2)
        old = jnp.where(r2 < 0.5, jnp.exp(jnp.minimum(inward - after, 0.0)), 0.0)
        new = jnp.exp(m2 - after)
        here = z == k
        em = jnp.where(here, after, em)
        e0 = jnp.where(here, old * n0 + new * p0, e0)
        e1 = jnp.where(here, old * n1 + new * p1, e1)
        gates[NZ + NY + k, 0:1, :] = old
        gates[NZ + NY + k, 1:2, :] = new

    inward = jnp.broadcast_to(em, (8, 128)) + decay
    fresh = seg < 0.5
    merged = jnp.where(fresh, jnp.maximum(inward, local_max), local_max)
    carried = jnp.where(fresh, jnp.exp(jnp.minimum(inward - merged, 0.0)), 0.0)
    own = jnp.exp(local_max - merged)
    carried_cols, own_cols = jnp.transpose(carried), jnp.transpose(own)
    en = jnp.concatenate([e0, e1], 1)
    high = en.astype(BF16)
    rest = en - high.astype(F32)
    mid = rest.astype(BF16)
    low = (rest - mid.astype(F32)).astype(BF16)
    norms = jnp.concatenate(
        [high.astype(F32), mid.astype(F32), low.astype(F32), jnp.zeros((5, DK), F32)], 0
    ).astype(BF16)
    sden = lax.dot_general(
        q_ref[...], norms, (((1,), (1,)), ((), ())), preferred_element_type=F32
    )
    sden = jnp.sum(sden, axis=1, keepdims=True)
    for i in range(8):
        rows = slice(i * 128, (i + 1) * 128)
        o, c = own_cols[:, i : i + 1], carried_cols[:, i : i + 1]
        whole = o * den[rows, :] + c * sden[rows, :]
        inverse = 1.0 / jnp.maximum(jnp.abs(whole), 1.0)
        den[rows, :] = c * inverse
        num[rows, :] = num[rows, :] * (o * inverse)

    def factor(j, kind):
        return jnp.concatenate([gates[j, kind : kind + 1, :]] * (DV // 128), 1)

    total(crecv, NZ - 1, crecv_sem).wait()
    part = jnp.zeros((DK // NZ, DV), F32)
    parts = []
    for k in range(NZ):
        parts.append(part)
        part = factor(k, 0) * part + factor(k, 1) * crecv[k].astype(F32)
    tpack[...] = part.astype(BF16)
    for dy in (1, 2, 3):
        remote(tpack, trecv.at[y], tsend, trecv_sem, at(y + dy, z), head).start()
    z_step(3, ())
    for k in (2, -2):
        f_sends(y, z - k, (), (1, -1))

    state = cmem_ref[pl.ds(pl.multiple_of(z * (DK // NZ), DK // NZ), DK // NZ), :]
    total(trecv, NY - 1, trecv_sem).wait()
    for row_at in range(NY - 1):
        joined = factor(NZ + row_at, 0) * state + factor(NZ + row_at, 1) * trecv[row_at].astype(F32)
        state = jnp.where(row_at < y, joined, state)
    for k in range(NZ):
        at_k = NZ + NY + k
        epack[k] = (factor(at_k, 0) * state + factor(at_k, 1) * parts[k]).astype(BF16)
    erecv[z] = epack[z]
    for d in range(1, NZ):
        to = (z + d) % NZ
        remote(epack.at[to], erecv.at[z], esend, erecv_sem, at(y, to), head).start()

    for k in (3, -3):
        f_sends(y, z - k, (), (1, -1))
    z_step(4)
    o_copy(y - 1, me).wait_recv()
    o_copy(y + 1, me).wait_recv()
    lift = z % 2 == 0
    o_copy(jnp.where(lift, y + 3, y + 1), at(jnp.where(lift, y + 1, y + 3), z)).start()

    y_step(-1, True)
    y_step(1, False)
    y_step(-2, False)
    y_step(2, True)
    total(erecv, NZ - 1, erecv_sem).wait()
    entry = erecv[...].reshape(DK, DV)
    mine, theirs = (x % 2) * 2 + core, (x % 2) * 2 + mate
    other, other_mate = (1 - x % 2) * 2 + core, (1 - x % 2) * 2 + mate

    def rows_of(t):
        return pl.ds(pl.multiple_of(t * XT, XT), XT)

    def h_copy(slot, t, hd):
        tile = hid.at[slot, rows_of(t)]
        return remote(tile, tile, hsend, hrecv.at[slot, t], me, hd)

    def make_hidden(t, c):
        rows = rows_of(t)
        qt = q_ref[rows, :]
        scale = den[rows, :]
        got = jnp.dot(qt, entry, preferred_element_type=F32)
        hid[mine, rows, :] = (num[rows, :] + scale * got).astype(BF16)
        h_copy(mine, t, near * 2 + core).start()
        h_copy(mine, t, x * 2 + mate).start()
        return c

    lax.fori_loop(0, NXT, make_hidden, 0)

    y_step(-3, True)
    y_step(3, False)
    y_step(-4, False)
    o_copy(y + 2, me).wait_recv()
    for a in (0, 1):
        for dz in (1, -1):
            r_copy(a, z, at(y, z + dz)).start()
    for o in range(-4, 4):
        f_copy(y + 2, z + o, me).wait_recv()

    def p_copy(t):
        return remote(
            part_out.at[rows_of(t)], part_in.at[rows_of(t)], psend, precv.at[t], me, far_head
        )

    def project(t, w_ref):
        whole = None
        for j in range(4):
            w = w_ref[8 * j : 8 * j + 8].reshape(DV, DV)
            term = jnp.dot(hid[j, rows_of(t), :], w, preferred_element_type=F32)
            whole = term if whole is None else whole + term
        return whole

    def ring_step(t):
        k, a = t // 2 + 1, t % 2

        @pl.when(k <= 4 - a)
        def _():
            r_copy(a, z - k, me).wait_recv()

        @pl.when(k <= 3 - a)
        def _():
            r_copy(a, z - k, at(y, z + 1)).start()

        @pl.when(k <= 3 + a)
        def _():
            r_copy(a, z + k, me).wait_recv()

        @pl.when(k <= 2 + a)
        def _():
            r_copy(a, z + k, at(y, z - 1)).start()

    def cross(t, c):
        h_copy(other, t, head).wait_recv()
        h_copy(other, t, x * 2 + mate).start()
        h_copy(theirs, t, head).wait_recv()
        h_copy(other_mate, t, head).wait_recv()
        part_out[rows_of(t), :] = project(t, wfar).astype(BF16)
        p_copy(t).start()
        ring_step(t)
        return c

    lax.fori_loop(0, NXT, cross, 0)

    def finish(t, c):
        kept = project(t, wown)
        p_copy(t).wait_recv()
        rows = rows_of(t)
        out_ref[rows, :] = (kept + part_in[rows, :].astype(F32)).astype(BF16)
        return c

    lax.fori_loop(0, NXT, finish, 0)

    total(wfar, 31, fsend).wait()
    total(wown, 31, osend).wait()
    total(stats, NZ - 1 + NY - 1, ssend).wait()
    total(cpack, NZ - 1, csend).wait()
    total(trecv, NY - 1, tsend).wait()
    total(epack, NZ - 1, esend).wait()
    total(hid, 3, hsend).wait()
    pltpu.make_async_copy(part_out, part_out, psend).wait()


def shards(q, k, v, ig, fg, ds, cmem, cnorm, cmax, w):
    dma = pltpu.SemaphoreType.DMA
    hbm = pl.BlockSpec(memory_space=pl.ANY)
    return pl.pallas_call(
        kernel,
        out_shape=pltpu.VMEM((TOK, DV), BF16),
        in_specs=[hbm] * 10,
        out_specs=pl.BlockSpec(memory_space=pltpu.VMEM),
        scratch_shapes=[
            pltpu.VMEM((TOK, DK), BF16),
            pltpu.VMEM((TOK, DK), BF16),
            pltpu.VMEM((TOK, DV), BF16),
            pltpu.VMEM((DK, DV), F32),
            pltpu.VMEM((8, 128), F32),
            pltpu.VMEM((8, 128), F32),
            pltpu.VMEM((8, 128), jnp.int32),
            pltpu.VMEM((2, 128), F32),
            pltpu.VMEM((1, 1), F32),
            pltpu.VMEM((NS, 64, DV), BF16),
            pltpu.VMEM((NS, 64, DV), BF16),
            pltpu.VMEM((NS, 8, 128), F32),
            pltpu.VMEM((NY, 8, 128), F32),
            pltpu.VMEM((NZ, DK // NZ, DV), BF16),
            pltpu.VMEM((NZ, DK // NZ, DV), BF16),
            pltpu.VMEM((DK // NZ, DV), BF16),
            pltpu.VMEM((NY, DK // NZ, DV), BF16),
            pltpu.VMEM((NZ, DK // NZ, DV), BF16),
            pltpu.VMEM((NZ, DK // NZ, DV), BF16),
            pltpu.VMEM((TOK, DV), F32),
            pltpu.VMEM((TOK, 1), F32),
            pltpu.VMEM((4, TOK, DV), BF16),
            pltpu.VMEM((TOK, DV), BF16),
            pltpu.VMEM((TOK, DV), BF16),
            pltpu.VMEM((NS, 8, 128), F32),
            dma((10,)), dma, dma((NS,)), dma, dma((NS,)), dma((16,)), dma, dma, dma, dma,
            dma, dma, dma, dma, dma, dma, dma, dma((4, NXT)), dma, dma((NXT,)),
        ],
        compiler_params=pltpu.CompilerParams(
            collective_id=0, has_side_effects=True, vmem_limit_bytes=60 * 2**20
        ),
    )(
        q, k, v, ig.reshape(8, 128), fg.reshape(8, 128), ds.reshape(8, 128),
        cmem.reshape(DK, DV), cnorm.reshape(2, 128), cmax.reshape(1, 1), w,
    )


def solution(mesh):
    placed = (
        P("seq", "head"),
        P("seq", "head"),
        P("seq", "head"),
        P("head", "seq"),
        P("head", "seq"),
        P("seq"),
        P("head", None, None),
        P("head", None),
        P("head"),
        P("seq", "head"),
    )
    return jax.shard_map(
        shards, mesh=mesh, in_specs=placed, out_specs=P("seq", "head"), check_vma=False
    )
```

```python
import jax
import jax.numpy as jnp
from jax import lax
from jax.experimental import pallas as pl
from jax.experimental.pallas import tpu as pltpu
from jax.sharding import PartitionSpec as P

DK = 256
DV = 512
TOK = 1024
NY, NZ = 4, 8
NS = NY * NZ
LOW = -1e30
MESH = pl.DeviceIdType.MESH
F32, BF16 = jnp.float32, jnp.bfloat16
QT = 256
XT = 128
NXT = TOK // XT


def lane_scan(a, op, fill, seg=None):
    lane = lax.broadcasted_iota(jnp.int32, a.shape, 1)
    for sh in (1, 2, 4, 8, 16, 32, 64):
        ok = lane >= sh
        if seg is not None:
            ok = ok & (pltpu.roll(seg, sh, 1) == seg)
        a = op(a, jnp.where(ok, pltpu.roll(a, sh, 1), fill))
    return a


def row_scan(a, op, fill, seg=None):
    row = lax.broadcasted_iota(jnp.int32, a.shape, 0)
    for sh in (1, 2, 4):
        ok = row >= sh
        if seg is not None:
            ok = ok & (pltpu.roll(seg, sh, 0) == seg)
        a = op(a, jnp.where(ok, pltpu.roll(a, sh, 0), fill))
    return a


def last_lane(a):
    return jnp.broadcast_to(a[:, 127:128], a.shape)


def before(a, fill):
    row = lax.broadcasted_iota(jnp.int32, a.shape, 0)
    return jnp.where(row >= 1, pltpu.roll(a, 1, 0), fill)


def running_sum(a):
    inside = lane_scan(a, jnp.add, 0.0)
    return inside + before(row_scan(last_lane(inside), jnp.add, 0.0), 0.0)


def running_max(a, seg):
    inside = lane_scan(a, jnp.maximum, LOW, seg)
    seg_end = last_lane(seg)
    ends = row_scan(last_lane(inside), jnp.maximum, LOW, seg_end)
    carried = jnp.where(before(seg_end, -1.0) == seg, before(ends, LOW), LOW)
    return jnp.maximum(inside, carried)


def column(cols, tile, size):
    per = size // 128
    return jnp.concatenate([cols[:, tile * per + i : tile * per + i + 1] for i in range(per)], 0)


def as_row(a, rows):
    return jnp.concatenate([a[i : i + 1, :] for i in range(rows)], 1)


def kernel(
    q_hbm, k_hbm, v_hbm, ig_hbm, fg_hbm, ds_hbm, cmem_hbm, cnorm_hbm, cmax_hbm, w_hbm,
    out_ref,
    q_ref, k_ref, v_ref, cmem_ref, ig_ref, fg_ref, ds_ref, cnorm_ref, cmax_ref,
    wfar, wown, stats, rowstats, cpack, crecv, tpack, trecv, epack, erecv, num, den, hid, part_out, part_in, gates,
    in_sem, fsend, frecv, osend, orecv, oring, swap_send, ssend, srecv, srecv_rows,
    csend, crecv_sem, tsend, trecv_sem, esend, erecv_sem, hsend, hrecv, psend, precv,
):
    me = lax.axis_index("seq")
    head = lax.axis_index("head")
    y, z = me // NZ, me % NZ
    x, core = head // 2, head % 2
    mate = 1 - core
    near = (x // 2) * 2 + (1 - x % 2)
    far = 3 - x
    home = (y // 2) == (x // 2)
    away = jnp.logical_not(home)
    opposite = (NY - 1 - y) * NZ + z
    far_head = far * 2 + core

    def at(yy, zz):
        return ((yy + NY) % NY) * NZ + (zz + NZ) % NZ

    barrier = pltpu.get_barrier_semaphore()

    def greet(seq, hd):
        pl.semaphore_signal(
            barrier, inc=1, device_id={"seq": seq, "head": hd}, device_id_type=MESH
        )

    for d in range(1, NZ):
        greet(at(y, z + d), head)
    for d in range(1, NY):
        greet(at(y + d, z), head)
    greet(me, x * 2 + mate)
    greet(me, near * 2 + core)
    greet(me, far_head)

    @pl.when(away)
    def _():
        greet(opposite, far_head)

    loads = [
        pltpu.make_async_copy(a, b, in_sem.at[i])
        for i, (a, b) in enumerate(
            (
                (fg_hbm, fg_ref), (ds_hbm, ds_ref), (ig_hbm, ig_ref), (k_hbm, k_ref),
                (v_hbm, v_ref), (q_hbm, q_ref), (cmem_hbm, cmem_ref), (cnorm_hbm, cnorm_ref),
                (cmax_hbm, cmax_ref),
            )
        )
    ]
    for load in loads:
        load.start()

    def remote(src, dst, send, recv, seq, hd):
        return pltpu.make_async_remote_copy(
            src_ref=src, dst_ref=dst, send_sem=send, recv_sem=recv,
            device_id={"seq": seq, "head": hd}, device_id_type=MESH,
        )

    def total(ref, count, sem):
        part = ref.at[pl.ds(0, count)]
        return pltpu.make_async_copy(part, part, sem)

    for i in range(3):
        loads[i].wait()
    lf = fg_ref[...]
    lf = jnp.minimum(lf, 0.0) - jnp.log1p(jnp.exp(-jnp.abs(lf)))
    decay = running_sum(lf)
    seg = running_sum(ds_ref[...].astype(F32))
    u = ig_ref[...] - decay
    top = running_max(u, seg)
    local_max = decay + top
    end = lambda a: jnp.broadcast_to(a[7:8, 127:128], (1, 128))
    seg_end = end(seg)
    coeff = jnp.where(seg == seg_end, jnp.exp(jnp.minimum(u - end(top), 0.0)), 0.0) * (DK**-0.5)
    coeff_cols = jnp.transpose(coeff)
    top_cols = jnp.transpose(top)
    seg_cols = jnp.transpose(seg)

    loads[3].wait()
    keyed = [
        k_ref[i * 128 : (i + 1) * 128, :].astype(F32) * coeff_cols[:, i : i + 1] for i in range(8)
    ]
    normal = sum(jnp.sum(t, axis=0, keepdims=True) for t in keyed)
    stats[me, 0:1, :] = normal[:, :128]
    stats[me, 1:2, :] = normal[:, 128:]
    stats[me, 2:3, :] = end(local_max)
    stats[me, 3:4, :] = end(decay)
    stats[me, 4:5, :] = jnp.where(seg_end > 0.5, 1.0, 0.0)
    pl.semaphore_wait(barrier, jnp.where(home, 13, 14))

    mine_row = (y % 2) * NZ + z
    upper, lower = w_hbm.at[pl.ds(0, 64)], w_hbm.at[pl.ds(64, 64)]
    first, second = 2 * mine_row, 2 * mine_row + 1
    stay = pltpu.make_async_copy(upper, wown.at[first], in_sem.at[9])

    @pl.when(home)
    def _():
        stay.start()
        remote(lower, wown.at[second], swap_send, orecv.at[opposite], opposite, head).start()

    @pl.when(away)
    def _():
        remote(upper, wfar.at[first], swap_send, frecv.at[me], me, far_head).start()
        remote(lower, wfar.at[second], swap_send, frecv.at[opposite], opposite, far_head).start()

    for d in range(1, NZ):
        remote(stats.at[me], stats.at[me], ssend, srecv, at(y, z + d), head).start()

    loads[4].wait()
    memory = lax.dot_general(
        jnp.concatenate([t.astype(BF16) for t in keyed], 0), v_ref[...],
        (((0,), (0,)), ((), ())), preferred_element_type=F32,
    ).astype(BF16)
    cpack[...] = memory.reshape(NZ, DK // NZ, DV)
    crecv[z] = cpack[z]
    for d in range(1, NZ):
        to = (z + d) % NZ
        remote(cpack.at[to], crecv.at[z], csend, crecv_sem, at(y, to), head).start()

    def place(yy, zz):
        yy = (yy + NY) % NY
        half = jnp.where((yy // 2) == (x // 2), 0, 1)
        return (((yy + half) % 2) * NZ + (zz + NZ) % NZ) * 2 + half

    def f_copy(yy, zz, dev):
        piece = wfar.at[place(yy, zz)]
        return remote(piece, piece, fsend, frecv.at[at(yy, zz)], dev, head)

    def o_copy(yy, dev):
        piece = wown.at[place(yy, z)]
        return remote(piece, piece, osend, orecv.at[at(yy, z)], dev, head)

    def r_copy(a, zz, dev):
        row = a * NZ + (zz + NZ) % NZ
        piece = wown.at[pl.ds(row * 2, 2)]
        return remote(piece, piece, osend, oring.at[row], dev, head)

    def f_sends(yy, zz, zs, ys):
        for dz in zs:
            f_copy(yy, zz, at(y, z + dz)).start()
        for dy in ys:
            f_copy(yy, zz, at(y + dy, z)).start()

    def z_step(k, ys=(1, -1)):
        f_copy(y, z - k, me).wait_recv()
        f_sends(y, z - k, (1,) if k <= 3 else (), ys)
        if k <= 3:
            f_copy(y, z + k, me).wait_recv()
            f_sends(y, z + k, (-1,) if k <= 2 else (), ys)

    def y_step(o, up):
        f_copy(y - 1, z + o, me).wait_recv()
        f_copy(y + 1, z + o, me).wait_recv()
        if up:
            f_sends(y - 1, z + o, (), (1,))
        else:
            f_sends(y + 1, z + o, (), (-1,))

    def attend(tile):
        n = (tile + 1) * QT
        qt = q_ref[tile * QT : (tile + 1) * QT, :]
        scores = lax.dot_general(
            qt, k_ref[:n, :], (((1,), (1,)), ((), ())), preferred_element_type=F32
        )
        blocks = n // 128
        u_row, seg_row = as_row(u, blocks), as_row(seg, blocks)
        spot = lax.broadcasted_iota(jnp.int32, (QT, n), 0) + tile * QT
        allowed = (lax.broadcasted_iota(jnp.int32, (QT, n), 1) <= spot) & (
            seg_row == column(seg_cols, tile, QT)
        )
        gain = jnp.exp(u_row - column(top_cols, tile, QT))
        weights = jnp.where(allowed, gain * (DK**-0.5), 0.0) * scores
        den[tile * QT : (tile + 1) * QT, :] = jnp.sum(weights, axis=1, keepdims=True)
        num[tile * QT : (tile + 1) * QT, :] = jnp.dot(
            weights.astype(BF16), v_ref[:n, :], preferred_element_type=F32
        )

    f_copy(y, z, me).wait_recv()
    f_sends(y, z, (1, -1), (1, -1))
    loads[5].wait()
    attend(0)
    total(stats, NZ - 1, srecv).wait()
    base = y * NZ
    m = jnp.full((1, 128), LOW, F32)
    g = r = n0 = n1 = jnp.zeros((1, 128), F32)
    prefixes = []
    for k in range(NZ):
        prefixes.append((m, g, r, n0, n1))
        m2, g2, r2 = (stats[base + k, c : c + 1, :] for c in (2, 3, 4))
        inward = m + g2
        m = jnp.where(r2 < 0.5, jnp.maximum(inward, m2), m2)
        old = jnp.where(r2 < 0.5, jnp.exp(jnp.minimum(inward - m, 0.0)), 0.0)
        new = jnp.exp(m2 - m)
        n0 = old * n0 + new * stats[base + k, 0:1, :]
        n1 = old * n1 + new * stats[base + k, 1:2, :]
        g, r = g + g2, jnp.maximum(r, r2)
        gates[k, 0:1, :] = old
        gates[k, 1:2, :] = new
    for c, value in enumerate((n0, n1, m, g, r)):
        rowstats[y, c : c + 1, :] = value
    for dy in (1, 2, 3):
        remote(
            rowstats.at[y], rowstats.at[y], ssend, srecv_rows, at(y + dy, z), head
        ).start()

    @pl.when(home)
    def _():
        stay.wait()
        remote(lower, wown.at[second], swap_send, orecv.at[opposite], opposite, head).wait_send()

    @pl.when(away)
    def _():
        pltpu.make_async_copy(w_hbm, w_hbm, swap_send).wait()
        o_copy(y, me).wait_recv()

    for dy in (1, -1):
        o_copy(y, at(y + dy, z)).start()
    z_step(1)
    attend(1)
    y_step(0, True)
    attend(2)
    z_step(2, ())
    attend(3)

    for i in (6, 7, 8):
        loads[i].wait()
    total(rowstats, NY - 1, srecv_rows).wait()
    m = jnp.broadcast_to(cmax_ref[...], (1, 128))
    n0, n1 = cnorm_ref[0:1, :], cnorm_ref[1:2, :]
    for row_at in range(NY - 1):
        m2, g2, r2 = (rowstats[row_at, c : c + 1, :] for c in (2, 3, 4))
        inward = m + g2
        after = jnp.where(r2 < 0.5, jnp.maximum(inward, m2), m2)
        old = jnp.where(r2 < 0.5, jnp.exp(jnp.minimum(inward - after, 0.0)), 0.0)
        new = jnp.exp(m2 - after)
        earlier = row_at < y
        n0 = jnp.where(earlier, old * n0 + new * rowstats[row_at, 0:1, :], n0)
        n1 = jnp.where(earlier, old * n1 + new * rowstats[row_at, 1:2, :], n1)
        m = jnp.where(earlier, after, m)
        gates[NZ + row_at, 0:1, :] = old
        gates[NZ + row_at, 1:2, :] = new
    em, e0, e1 = m, n0, n1
    for k in range(NZ):
        m2, g2, r2, p0, p1 = prefixes[k]
        inward = m + g2
        after = jnp.where(r2 < 0.5, jnp.maximum(inward, m2), m2)
        old = jnp.where(r2 < 0.5, jnp.exp(jnp.minimum(inward - after, 0.0)), 0.0)
        new = jnp.exp(m2 - after)
        here = z == k
        em = jnp.where(here, after, em)
        e0 = jnp.where(here, old * n0 + new * p0, e0)
        e1 = jnp.where(here, old * n1 + new * p1, e1)
        gates[NZ + NY + k, 0:1, :] = old
        gates[NZ + NY + k, 1:2, :] = new

    inward = jnp.broadcast_to(em, (8, 128)) + decay
    fresh = seg < 0.5
    merged = jnp.where(fresh, jnp.maximum(inward, local_max), local_max)
    carried = jnp.where(fresh, jnp.exp(jnp.minimum(inward - merged, 0.0)), 0.0)
    own = jnp.exp(local_max - merged)
    carried_cols, own_cols = jnp.transpose(carried), jnp.transpose(own)
    en = jnp.concatenate([e0, e1], 1)
    high = en.astype(BF16)
    rest = en - high.astype(F32)
    mid = rest.astype(BF16)
    low = (rest - mid.astype(F32)).astype(BF16)
    norms = jnp.concatenate(
        [high.astype(F32), mid.astype(F32), low.astype(F32), jnp.zeros((5, DK), F32)], 0
    ).astype(BF16)
    sden = lax.dot_general(
        q_ref[...], norms, (((1,), (1,)), ((), ())), preferred_element_type=F32
    )
    sden = jnp.sum(sden, axis=1, keepdims=True)
    for i in range(8):
        rows = slice(i * 128, (i + 1) * 128)
        o, c = own_cols[:, i : i + 1], carried_cols[:, i : i + 1]
        whole = o * den[rows, :] + c * sden[rows, :]
        inverse = 1.0 / jnp.maximum(jnp.abs(whole), 1.0)
        den[rows, :] = c * inverse
        num[rows, :] = num[rows, :] * (o * inverse)

    def factor(j, kind):
        return jnp.concatenate([gates[j, kind : kind + 1, :]] * (DV // 128), 1)

    total(crecv, NZ - 1, crecv_sem).wait()
    part = jnp.zeros((DK // NZ, DV), F32)
    parts = []
    for k in range(NZ):
        parts.append(part)
        part = factor(k, 0) * part + factor(k, 1) * crecv[k].astype(F32)
    tpack[...] = part.astype(BF16)
    for dy in (1, 2, 3):
        remote(tpack, trecv.at[y], tsend, trecv_sem, at(y + dy, z), head).start()
    z_step(3, ())
    for k in (2, -2):
        f_sends(y, z - k, (), (1, -1))

    state = cmem_ref[pl.ds(pl.multiple_of(z * (DK // NZ), DK // NZ), DK // NZ), :]
    total(trecv, NY - 1, trecv_sem).wait()
    for row_at in range(NY - 1):
        joined = factor(NZ + row_at, 0) * state + factor(NZ + row_at, 1) * trecv[row_at].astype(F32)
        state = jnp.where(row_at < y, joined, state)
    for k in range(NZ):
        at_k = NZ + NY + k
        epack[k] = (factor(at_k, 0) * state + factor(at_k, 1) * parts[k]).astype(BF16)
    erecv[z] = epack[z]
    for d in range(1, NZ):
        to = (z + d) % NZ
        remote(epack.at[to], erecv.at[z], esend, erecv_sem, at(y, to), head).start()

    for k in (3, -3):
        f_sends(y, z - k, (), (1, -1))
    y_step(-1, True)
    y_step(1, False)
    z_step(4)
    o_copy(y - 1, me).wait_recv()
    o_copy(y + 1, me).wait_recv()
    lift = z % 2 == 0
    o_copy(jnp.where(lift, y + 3, y + 1), at(jnp.where(lift, y + 1, y + 3), z)).start()

    y_step(-2, False)
    y_step(2, True)
    total(erecv, NZ - 1, erecv_sem).wait()
    entry = erecv[...].reshape(DK, DV)
    mine, theirs = (x % 2) * 2 + core, (x % 2) * 2 + mate
    other, other_mate = (1 - x % 2) * 2 + core, (1 - x % 2) * 2 + mate

    def rows_of(t):
        return pl.ds(pl.multiple_of(t * XT, XT), XT)

    def h_copy(slot, t, hd):
        tile = hid.at[slot, rows_of(t)]
        return remote(tile, tile, hsend, hrecv.at[slot, t], me, hd)

    def make_hidden(t, c):
        rows = rows_of(t)
        qt = q_ref[rows, :]
        scale = den[rows, :]
        got = jnp.dot(qt, entry, preferred_element_type=F32)
        hid[mine, rows, :] = (num[rows, :] + scale * got).astype(BF16)
        h_copy(mine, t, near * 2 + core).start()
        h_copy(mine, t, x * 2 + mate).start()
        return c

    lax.fori_loop(0, NXT, make_hidden, 0)

    y_step(-3, True)
    y_step(3, False)
    y_step(-4, False)
    o_copy(y + 2, me).wait_recv()
    for a in (0, 1):
        for dz in (1, -1):
            r_copy(a, z, at(y, z + dz)).start()
    for o in range(-4, 4):
        f_copy(y + 2, z + o, me).wait_recv()

    def p_copy(t):
        return remote(
            part_out.at[rows_of(t)], part_in.at[rows_of(t)], psend, precv.at[t], me, far_head
        )

    def project(t, w_ref):
        whole = None
        for j in range(4):
            w = w_ref[8 * j : 8 * j + 8].reshape(DV, DV)
            term = jnp.dot(hid[j, rows_of(t), :], w, preferred_element_type=F32)
            whole = term if whole is None else whole + term
        return whole

    def ring_step(t):
        k, a = t // 2 + 1, t % 2

        @pl.when(k <= 4 - a)
        def _():
            r_copy(a, z - k, me).wait_recv()

        @pl.when(k <= 3 - a)
        def _():
            r_copy(a, z - k, at(y, z + 1)).start()

        @pl.when(k <= 3 + a)
        def _():
            r_copy(a, z + k, me).wait_recv()

        @pl.when(k <= 2 + a)
        def _():
            r_copy(a, z + k, at(y, z - 1)).start()

    def cross(t, c):
        h_copy(other, t, head).wait_recv()
        h_copy(other, t, x * 2 + mate).start()
        h_copy(theirs, t, head).wait_recv()
        h_copy(other_mate, t, head).wait_recv()
        part_out[rows_of(t), :] = project(t, wfar).astype(BF16)
        p_copy(t).start()
        ring_step(t)
        return c

    lax.fori_loop(0, NXT, cross, 0)

    def finish(t, c):
        kept = project(t, wown)
        p_copy(t).wait_recv()
        rows = rows_of(t)
        out_ref[rows, :] = (kept + part_in[rows, :].astype(F32)).astype(BF16)
        return c

    lax.fori_loop(0, NXT, finish, 0)

    total(wfar, 31, fsend).wait()
    total(wown, 31, osend).wait()
    total(stats, NZ - 1 + NY - 1, ssend).wait()
    total(cpack, NZ - 1, csend).wait()
    total(trecv, NY - 1, tsend).wait()
    total(epack, NZ - 1, esend).wait()
    total(hid, 3, hsend).wait()
    pltpu.make_async_copy(part_out, part_out, psend).wait()


def shards(q, k, v, ig, fg, ds, cmem, cnorm, cmax, w):
    dma = pltpu.SemaphoreType.DMA
    hbm = pl.BlockSpec(memory_space=pl.ANY)
    return pl.pallas_call(
        kernel,
        out_shape=pltpu.VMEM((TOK, DV), BF16),
        in_specs=[hbm] * 10,
        out_specs=pl.BlockSpec(memory_space=pltpu.VMEM),
        scratch_shapes=[
            pltpu.VMEM((TOK, DK), BF16),
            pltpu.VMEM((TOK, DK), BF16),
            pltpu.VMEM((TOK, DV), BF16),
            pltpu.VMEM((DK, DV), F32),
            pltpu.VMEM((8, 128), F32),
            pltpu.VMEM((8, 128), F32),
            pltpu.VMEM((8, 128), jnp.int32),
            pltpu.VMEM((2, 128), F32),
            pltpu.VMEM((1, 1), F32),
            pltpu.VMEM((NS, 64, DV), BF16),
            pltpu.VMEM((NS, 64, DV), BF16),
            pltpu.VMEM((NS, 8, 128), F32),
            pltpu.VMEM((NY, 8, 128), F32),
            pltpu.VMEM((NZ, DK // NZ, DV), BF16),
            pltpu.VMEM((NZ, DK // NZ, DV), BF16),
            pltpu.VMEM((DK // NZ, DV), BF16),
            pltpu.VMEM((NY, DK // NZ, DV), BF16),
            pltpu.VMEM((NZ, DK // NZ, DV), BF16),
            pltpu.VMEM((NZ, DK // NZ, DV), BF16),
            pltpu.VMEM((TOK, DV), F32),
            pltpu.VMEM((TOK, 1), F32),
            pltpu.VMEM((4, TOK, DV), BF16),
            pltpu.VMEM((TOK, DV), BF16),
            pltpu.VMEM((TOK, DV), BF16),
            pltpu.VMEM((NS, 8, 128), F32),
            dma((10,)), dma, dma((NS,)), dma, dma((NS,)), dma((16,)), dma, dma, dma, dma,
            dma, dma, dma, dma, dma, dma, dma, dma((4, NXT)), dma, dma((NXT,)),
        ],
        compiler_params=pltpu.CompilerParams(
            collective_id=0, has_side_effects=True, vmem_limit_bytes=60 * 2**20
        ),
    )(
        q, k, v, ig.reshape(8, 128), fg.reshape(8, 128), ds.reshape(8, 128),
        cmem.reshape(DK, DV), cnorm.reshape(2, 128), cmax.reshape(1, 1), w,
    )


def solution(mesh):
    placed = (
        P("seq", "head"),
        P("seq", "head"),
        P("seq", "head"),
        P("head", "seq"),
        P("head", "seq"),
        P("seq"),
        P("head", None, None),
        P("head", None),
        P("head"),
        P("seq", "head"),
    )
    return jax.shard_map(
        shards, mesh=mesh, in_specs=placed, out_specs=P("seq", "head"), check_vma=False
    )
```
